256 devices in a mesh: mp: 8 (over z_lo, core), seq: 32 (over x, z_hi, y).
Axes of the slice: x: 4, y: 4, z: 8 (z_hi: 2, z_lo: 4; z = z_hi * 4 + z_lo), core: 2. Of those that a mesh axis runs over, the one named last changes fastest.
Arguments:
- noise_gen: bfloat16 [8, 1024, 64], P('mp', 'seq'), may hold values from -6 to 6
- noise_add: bfloat16 [8, 1024, 64], P('mp', 'seq'), may hold values from -6 to 6
- steps_t: int32 [4], replicated, may hold values from 20 to 979
- gen_in: bfloat16 [64, 5120], replicated, may hold values from -0.75 to 0.75
- gen_out: bfloat16 [5120, 64], replicated, may hold values from -0.078125 to 0.078125
- real_in: bfloat16 [64, 5120], replicated, may hold values from -0.75 to 0.75
- real_qkv: bfloat16 [5120, 3, 32, 128], P('mp', None, 'seq'), may hold values from -2.5 to 2.5
- real_proj: bfloat16 [32, 128, 5120], P('seq', None, 'mp'), may hold values from -0.09375 to 0.09375
- real_head: bfloat16 [5120, 64], replicated, may hold values from -0.078125 to 0.078125
- fake_in: bfloat16 [64, 5120], replicated, may hold values from -0.75 to 0.75
- fake_qkv: bfloat16 [5120, 3, 32, 128], P('mp', None, 'seq'), may hold values from -2.5 to 2.5
- fake_proj: bfloat16 [32, 128, 5120], P('seq', None, 'mp'), may hold values from -0.09375 to 0.09375
- fake_head: bfloat16 [5120, 64], replicated, may hold values from -0.078125 to 0.078125
Outputs:
- dmd_grad: float32 [8, 1024, 64], P('mp', 'seq')
- grad_in: float32 [64, 5120], P(None, 'seq')
- grad_out: float32 [5120, 64], P('seq')
The draws below stay inside these ranges and needn't reach their ends.
All inputs are finite; a program needn't handle non-finite values.
Results may differ from the reference program's by a relative error of at most 0.01.
Values may be sent and summed in bfloat16 or wider, within the bound.
A program may use at most 128 MiB of HBM per device.

```python
import math
import jax
import jax.numpy as jnp
from jax import lax

P_SIZE = 64
D = 5120
HEADS = 32
HS = 128
HALF = 32
LENGTH = 2048
CLIPS = 4
N_MP = 8
N_SEQ = 32


def normal_table(key):
    return jax.random.normal(key, (D, 3, HEADS, HS), jnp.float32) * D ** (-0.5)


def draw_real_qkv(key, part):
    key = jax.random.fold_in(key, 11)
    table = normal_table(key)
    return jnp.clip(table, -2.5, 2.5).astype(jnp.bfloat16)


def draw_fake_qkv(key, part):
    key = jax.random.fold_in(key, 23)
    table = normal_table(key)
    return jnp.clip(table, -2.5, 2.5).astype(jnp.bfloat16)


def plant(entries, key, least, largest):
    place = [jax.random.randint(jax.random.fold_in(key, axis), (), 0, length) for axis, length in enumerate(entries.shape)]
    longest = entries.shape.index(max(entries.shape))
    next_to = place[:longest] + [(place[longest] + 1) % entries.shape[longest]] + place[longest + 1:]
    return entries.at[tuple(place)].set(least).at[tuple(next_to)].set(largest)


def shard_levels(own_key, shape, pieces, low, top_value):
    gain, own = 1.0, jax.random.fold_in(own_key, 6)
    for position, shards_of in pieces:
        draws = jnp.exp(jax.random.uniform(jax.random.fold_in(own, position), (shards_of,), jnp.float32, low / len(pieces), top_value / len(pieces)))
        gain = gain * jnp.repeat(draws, shape[position] // shards_of).reshape([-1 if axis == position else 1 for axis in range(len(shape))])
    return gain


def gaussian(own_key, shape, scale, reach, cuts=(), kind=jnp.bfloat16):
    gain = shard_levels(own_key, shape, cuts, -0.22, 0.18) if cuts else 1.0
    values = jax.random.normal(own_key, shape, jnp.float32) * scale * gain
    return jnp.minimum(jnp.maximum(values, -reach), reach).astype(kind)


def setup_inputs(seed: int = 0) -> dict:
    seeds = jax.random.split(jax.random.key(seed), 14)
    return {
        "noise_gen": gaussian(seeds[0], (N_MP, LENGTH // 2, P_SIZE), 1.0, 6.0, ((0, 8), (1, 32))),
        "noise_add": gaussian(seeds[1], (N_MP, LENGTH // 2, P_SIZE), 1.0, 6.0, ((0, 8), (1, 32))),
        "steps_t": plant(jax.random.randint(seeds[2], (CLIPS,), 20, 980), jax.random.fold_in(seeds[2], 1), 20, 979).astype(jnp.int32),
        "gen_in": gaussian(seeds[3], (P_SIZE, D), P_SIZE ** -0.5, 0.75),
        "gen_out": gaussian(seeds[4], (D, P_SIZE), D ** -0.5, 0.078125),
        "real_in": gaussian(seeds[5], (P_SIZE, D), P_SIZE ** -0.5, 0.75),
        "real_qkv": draw_real_qkv(jax.random.fold_in(seeds[13], 71), 0),
        "real_proj": gaussian(seeds[7], (HEADS, HS, D), (HEADS * HS) ** -0.5, 0.09375, ((0, 32), (2, 8))),
        "real_head": gaussian(seeds[8], (D, P_SIZE), D ** -0.5, 0.078125),
        "fake_in": gaussian(seeds[9], (P_SIZE, D), P_SIZE ** -0.5, 0.75),
        "fake_qkv": draw_fake_qkv(jax.random.fold_in(seeds[13], 71), 0),
        "fake_proj": gaussian(seeds[11], (HEADS, HS, D), (HEADS * HS) ** -0.5, 0.09375, ((0, 32), (2, 8))),
        "fake_head": gaussian(seeds[12], (D, P_SIZE), D ** -0.5, 0.078125),
    }


def attend_head(queries, keys_all, values_all):
    scores = jnp.dot(queries.astype(jnp.float32), keys_all.astype(jnp.float32).T) / math.sqrt(HS)
    row_max = lax.optimization_barrier(jnp.max(scores, axis=-1, keepdims=True))
    weights = jnp.exp(scores - row_max)
    probs = (weights / lax.optimization_barrier(jnp.sum(weights, axis=-1, keepdims=True))).astype(jnp.bfloat16)
    return jnp.dot(probs.astype(jnp.float32), values_all.astype(jnp.float32)).astype(jnp.bfloat16)

def score_model(sequence, embed, table, proj, head):
    stream_in = jnp.dot(sequence, embed, preferred_element_type=jnp.float32).astype(jnp.bfloat16)
    packed = jnp.einsum('td,dcnh->ncth', stream_in.astype(jnp.float32), table.astype(jnp.float32)).astype(jnp.bfloat16)
    attended = lax.map(lambda heads: attend_head(heads[0], heads[1], heads[2]), packed)
    branch = jnp.einsum('nth,nhd->td', attended.astype(jnp.float32), proj.astype(jnp.float32))
    stream_out = stream_in.astype(jnp.float32) + branch
    return jnp.dot(stream_out, head.astype(jnp.float32), precision=lax.Precision.HIGHEST)

def reference(noise_gen, noise_add, steps_t, gen_in, gen_out, real_in, real_qkv, real_proj, real_head, fake_in, fake_qkv, fake_proj, fake_head):
    flat_noise = noise_gen.reshape(-1, P_SIZE)
    pre_act = jnp.dot(flat_noise, gen_in, preferred_element_type=jnp.float32)
    hidden = jax.nn.silu(pre_act).astype(jnp.bfloat16)
    clean_guess = flat_noise.astype(jnp.float32) + jnp.dot(hidden, gen_out, preferred_element_type=jnp.float32)
    level_rows = jnp.repeat(steps_t.astype(jnp.float32) / 1000.0, 2)
    level_flat = jnp.repeat(level_rows, LENGTH // 2)[:, None]
    noised = ((1.0 - level_flat) * clean_guess + level_flat * noise_add.reshape(-1, P_SIZE).astype(jnp.float32)).astype(jnp.bfloat16)
    noised_rows = noised.reshape(N_MP, N_SEQ, HALF, P_SIZE)
    real_rows = []
    fake_rows = []
    for clip_number in range(CLIPS):
        pair_rows = noised_rows[2 * clip_number:2 * clip_number + 2]
        sequence = pair_rows.transpose(1, 0, 2, 3).reshape(LENGTH, P_SIZE)
        for weights, store in (((real_in, real_qkv, real_proj, real_head), real_rows), ((fake_in, fake_qkv, fake_proj, fake_head), fake_rows)):
            velocity = score_model(sequence, weights[0], weights[1], weights[2], weights[3])
            velocity = velocity.reshape(N_SEQ, 2, HALF, P_SIZE).transpose(1, 0, 2, 3).reshape(2, LENGTH // 2, P_SIZE)
            store.append(velocity)
    velocity_real = jnp.concatenate(real_rows, axis=0)
    velocity_fake = jnp.concatenate(fake_rows, axis=0)
    dmd_grad = level_rows[:, None, None] * (velocity_real - velocity_fake)
    loss_scale = 1.0 / math.sqrt(CLIPS * LENGTH)
    scaled = (dmd_grad.reshape(-1, P_SIZE) * loss_scale).astype(jnp.bfloat16)
    grad_out = jnp.dot(hidden.T, scaled, preferred_element_type=jnp.float32)
    back_hidden = jnp.dot(scaled, gen_out.T, preferred_element_type=jnp.float32)
    sigmoid_pre = jax.nn.sigmoid(pre_act)
    pre_grad = (back_hidden * sigmoid_pre * (1.0 + pre_act * (1.0 - sigmoid_pre))).astype(jnp.bfloat16)
    grad_in = jnp.dot(flat_noise.T, pre_grad, preferred_element_type=jnp.float32)
    return (dmd_grad, grad_in, grad_out)
```

```python
import functools
import math

import jax
import jax.numpy as jnp
from jax import lax
from jax.experimental import pallas as pl
from jax.experimental.pallas import tpu as pltpu
from jax.sharding import PartitionSpec as P

MESH = pl.DeviceIdType.MESH
F32 = jnp.float32
BF16 = jnp.bfloat16
NN = (((1,), (0,)), ((), ()))
NT = (((1,), (1,)), ((), ()))
HIGH = lax.Precision.HIGHEST
SCORE_SCALE = math.log2(math.e) / math.sqrt(128.0)
LOSS_SCALE = 1.0 / math.sqrt(8192.0)


def mm(a, b, dims=NN, precision=None):
    return lax.dot_general(a, b, dims, precision=precision, preferred_element_type=F32)


def lanes(shape):
    return lax.broadcasted_iota(jnp.int32, shape, len(shape) - 1)


def roll(value, shift):
    return pltpu.roll(value, shift, 1)


def fold(square):
    return jnp.concatenate([square[0:32], square[32:64]], axis=1)


def kernel(
    steps,
    noise_gen,
    noise_add,
    gen_in,
    gen_out,
    real_in,
    real_qkv,
    real_proj,
    real_head,
    fake_in,
    fake_qkv,
    fake_proj,
    fake_head,
    dmd_out,
    gin_out,
    gout_out,
    gin_v,
    gout_v,
    emb_v,
    head_v,
    qkv_v,
    proj_v,
    embs_v,
    heads_v,
    job_send,
    job_recv,
    ac,
    msg,
    msg_r,
    tok,
    noi,
    keys_t,
    vals,
    hid,
    dsil,
    vel,
    vel_r,
    sca,
    gpart,
    grecv,
    fin,
    load_sem,
    job_ssem,
    job_rsem,
    z_ssem,
    z_rsem,
    ac_ssem,
    ac_rsem,
    core_ssem,
    core_rsem,
    tokz_ssem,
    tokz_rsem,
    tok_ssem,
    tok_rsem,
    noi_ssem,
    noi_rsem,
    sca_ssem,
    sca_rsem,
    g_ssem,
    g_rsem,
):
    mp = lax.axis_index("mp")
    seq = lax.axis_index("seq")
    core = mp % 2
    zlo = mp // 2
    x = seq // 8
    zhi = (seq // 4) % 2
    y = seq % 4
    me_p = x * 4 + y

    def dev(x_, y_, zhi_, zlo_, core_):
        return (zlo_ * 2 + core_, x_ * 8 + zhi_ * 4 + y_)

    def plane_dev(k):
        return dev((x + k // 4) % 4, (y + k % 4) % 4, zhi, zlo, core)

    partner = dev(x, y, zhi, zlo, 1 - core)
    across = dev(x, y, 1 - zhi, zlo, core)

    def rc(src, dst, ssem, rsem, device):
        return pltpu.make_async_remote_copy(
            src_ref=src, dst_ref=dst, send_sem=ssem, recv_sem=rsem, device_id=device, device_id_type=MESH
        )

    def to_plane(src, dst, ssem, rsem):
        def send(k, carry):
            rc(src, dst, ssem, rsem, plane_dev(k)).start()
            return carry

        lax.fori_loop(1, 16, send, 0)

    def got(ref, rsem):
        rc(ref, ref, rsem, rsem, partner).wait_recv()

    def sent(ref, ssem):
        rc(ref, ref, ssem, ssem, partner).wait_send()

    row = pl.ds(pl.multiple_of(mp * 640, 128), 640)
    loads = [
        pltpu.make_async_copy(real_in.at[:, row], embs_v.at[0], load_sem.at[0]),
        pltpu.make_async_copy(real_qkv, qkv_v.at[0], load_sem.at[1]),
        pltpu.make_async_copy(real_head.at[:, row], heads_v.at[0], load_sem.at[2]),
        pltpu.make_async_copy(real_proj, proj_v.at[0], load_sem.at[3]),
        pltpu.make_async_copy(fake_in.at[:, row], embs_v.at[1], load_sem.at[4]),
        pltpu.make_async_copy(fake_qkv, qkv_v.at[1], load_sem.at[5]),
        pltpu.make_async_copy(fake_head.at[:, row], heads_v.at[1], load_sem.at[6]),
        pltpu.make_async_copy(fake_proj, proj_v.at[1], load_sem.at[7]),
        pltpu.make_async_copy(gen_in, gin_v, load_sem.at[8]),
        pltpu.make_async_copy(gen_out, gout_v, load_sem.at[9]),
    ]
    for load in loads:
        load.start()

    @pl.when(core == 0)
    def _():
        pltpu.make_async_copy(real_in, emb_v, load_sem.at[10]).start()
        pltpu.make_async_copy(real_head, head_v, load_sem.at[11]).start()

    @pl.when(core == 1)
    def _():
        pltpu.make_async_copy(fake_in, emb_v, load_sem.at[10]).start()
        pltpu.make_async_copy(fake_head, head_v, load_sem.at[11]).start()

    barrier = pltpu.get_barrier_semaphore()

    def greet(device):
        pl.semaphore_signal(barrier, inc=1, device_id=device, device_id_type=MESH)

    def greet_plane(k, carry):
        greet(plane_dev(k))
        return carry

    def greet_mp(k, carry):
        greet(((mp + k) % 8, seq))
        return carry

    def greet_across(k, carry):
        greet(dev(x, y, 1 - zhi, k, core))
        return carry

    lax.fori_loop(1, 8, greet_mp, 0)
    lax.fori_loop(0, 4, greet_across, 0)
    lax.fori_loop(1, 16, greet_plane, 0)

    for m in range(2):
        for k in range(4):
            loads[4 * m + k].wait()
        for c in range(3):
            job_send[2 * m + c // 2, :, (c % 2) * 128 : (c % 2) * 128 + 128] = mm(embs_v[m], qkv_v[m, c]).astype(BF16)
        job_send[2 * m + 1, :, 128:256] = mm(heads_v[m], proj_v[m], NT).astype(BF16)

    level = steps[zlo].astype(F32) / 1000.0
    loads[8].wait()
    loads[9].wait()
    own_noise = noise_gen[...]
    clean = own_noise.astype(F32)
    for c in range(5):
        cols = slice(c * 1024, c * 1024 + 1024)
        u = mm(own_noise, gin_v[:, cols])
        hidden = (u * jax.nn.sigmoid(u)).astype(BF16)
        clean = clean + mm(hidden, gout_v[:, cols], NT)
    noised = (1.0 - level) * clean + level * noise_add[...].astype(F32)
    msg[...] = jnp.concatenate([noised, own_noise.astype(F32)], axis=1).astype(BF16)

    pl.semaphore_wait(barrier, 26)

    for m in range(2):
        for t in range(2):

            @pl.when(jnp.logical_not((zlo == 1 + t) & (core == m)))
            def _(m=m, t=t):
                rc(
                    job_send.at[2 * m + t],
                    job_recv.at[mp],
                    job_ssem.at[2 * m + t],
                    job_rsem.at[mp],
                    dev(x, y, zhi, 1 + t, m),
                ).start()

    rc(msg, msg_r, core_ssem.at[0], core_rsem.at[0], partner).start()
    got(msg_r, core_rsem.at[0])
    left = lanes((32, 128)) < 64
    mine = msg[...].astype(F32)
    other = msg_r[...].astype(F32)
    half0 = jnp.where(core == 0, mine, other)
    half1 = jnp.where(core == 0, other, mine)
    own_tok = jnp.where(left, half0, roll(half1, 64))
    tok[zhi, me_p] = own_tok.astype(BF16)
    noi[me_p] = jnp.where(left, roll(half0, 64), half1).astype(BF16)
    own_ref = tok.at[zhi, me_p]
    rc(own_ref, own_ref, tokz_ssem, tokz_rsem, across).start()
    to_plane(own_ref, own_ref, tok_ssem, tok_rsem)
    xtok = jnp.concatenate([own_tok[:, 0:64], own_tok[:, 64:128]], axis=0)
    xfold = jnp.concatenate([xtok[:, 0:32], xtok[:, 32:64]], axis=0).astype(BF16)
    xtok = xtok.astype(BF16)

    pltpu.make_async_copy(real_in, emb_v, load_sem.at[10]).wait()
    pltpu.make_async_copy(real_head, head_v, load_sem.at[11]).wait()
    direct = mm(emb_v[...], head_v[...], NT)
    vel[...] = mm(xtok.astype(F32), direct, precision=HIGH)

    t_here = zlo - 1
    slot_here = zhi * 2 + t_here

    @pl.when((zlo == 1) | (zlo == 2))
    def _():
        total = job_send[core * 2 + t_here].astype(F32)
        for src in range(8):

            @pl.when(src != mp)
            def _(src=src):
                got(job_recv.at[src], job_rsem.at[src])

            @pl.when(src == mp)
            def _(src=src):
                job_recv[src] = jnp.zeros((64, 256), BF16)

            total = total + job_recv[src].astype(F32)
        scale = jnp.where(t_here == 0, SCORE_SCALE, 1.0).astype(F32)
        square = mm(total[:, 0:128], total[:, 128:256], NT, HIGH) * scale
        ac[me_p, slot_here] = fold(square).astype(BF16)
        piece = ac.at[me_p, slot_here]

        def spread(k, carry):
            z = (zhi * 4 + zlo + k) % 8
            rc(piece, piece, z_ssem, z_rsem.at[slot_here], dev(x, y, z // 4, z % 4, core)).start()
            return carry

        lax.fori_loop(1, 8, spread, 0)

    far_ref = tok.at[1 - zhi, me_p]
    got(far_ref, tokz_rsem)
    to_plane(far_ref, far_ref, tok_ssem, tok_rsem)

    for order in range(4):
        group = zhi if order < 2 else 1 - zhi
        slot = group * 2 + order % 2
        piece = ac.at[me_p, slot]

        @pl.when(jnp.logical_not((group == zhi) & (zlo == 1 + order % 2)))
        def _(piece=piece, slot=slot):
            got(piece, z_rsem.at[slot])

        to_plane(piece, piece, ac_ssem, ac_rsem.at[me_p])

    noi_ref = noi.at[me_p]
    to_plane(noi_ref, noi_ref, noi_ssem, noi_rsem)

    got(tok.at[0:2, 0:15], tok_rsem)
    for g in range(2):
        block = tok[g].reshape(512, 128).astype(F32)
        flipped = block.T.astype(BF16)
        keys_t[:, g * 512 : g * 512 + 512] = flipped[0:64]
        keys_t[:, 1024 + g * 512 : 1024 + g * 512 + 512] = flipped[64:128]
        near = lanes((512, 128)) < 64
        vals[g * 512 : g * 512 + 512, :] = jnp.where(near, block, 1.0).astype(BF16)
        vals[1024 + g * 512 : 1024 + g * 512 + 512, :] = jnp.where(near, roll(block, 64), 1.0).astype(BF16)

    def attend(b, acc):
        spots = []
        for e in range(2):
            k = 2 * b + e
            spot = ((x + k // 4) % 4) * 4 + (y + k % 4) % 4
            spots.append(spot)

            @pl.when(k > 0)
            def _(spot=spot):
                got(ac.at[spot], ac_rsem.at[spot])

        mats = jnp.concatenate([ac[spots[e], 2 * g] for e in range(2) for g in range(2)], axis=1)
        both = mm(xfold, mats)
        queries = jnp.concatenate(
            [
                both[0:64, i * 128 : i * 128 + 64] + both[64:128, i * 128 + 64 : i * 128 + 128]
                for i in range(4)
            ],
            axis=0,
        ).astype(BF16)
        scores = mm(queries, keys_t[...])
        top = jnp.max(scores, axis=1, keepdims=True)
        weights = jnp.exp2(scores - top).astype(BF16)
        mixed = mm(weights, vals[...])
        heads = (mixed[:, 0:64] / mixed[:, 64:128]).astype(BF16)
        for i in range(4):
            part = heads[i * 64 : i * 64 + 64]
            folded = jnp.concatenate([part[:, 0:32], part[:, 32:64]], axis=0)
            acc = acc + mm(folded, ac[spots[i // 2], 2 * (i % 2) + 1])
        return acc

    acc = lax.fori_loop(0, 8, attend, jnp.zeros((128, 128), F32))
    total_vel = vel[...] + acc[0:64, 0:64] + acc[64:128, 64:128]
    vel_fold = jnp.concatenate([total_vel[0:32], total_vel[32:64]], axis=1)
    sca_f = vel_fold
    fin[0:32, :] = sca_f
    rc(fin.at[0:32], vel_r, core_ssem.at[1], core_rsem.at[1], partner).start()

    got(noi.at[0:15], noi_rsem)
    col0 = 160 * (x * 8 + core * 4 + y)
    base = pl.ds(pl.multiple_of((col0 // 128) * 128, 128), 256)
    shift = 256 - 32 * y
    gin_s = pltpu.roll(gin_v[:, base].astype(F32), shift, 1).astype(BF16)
    gout_s = pltpu.roll(gout_v[:, base].astype(F32), shift, 1).astype(BF16)
    zeros = jnp.zeros((64, 256), BF16)
    noise_rows = noi[...].reshape(512, 128)
    for h in range(2):
        weight = jnp.concatenate([gin_s, zeros] if h == 0 else [zeros, gin_s], axis=0)
        u = mm(noise_rows, weight)
        sig = jax.nn.sigmoid(u)
        hid[h] = (u * sig).astype(BF16)
        dsil[h] = sig * (1.0 + u * (1.0 - sig))
    noise_t = noise_rows.astype(F32).T.astype(BF16)

    got(vel_r, core_rsem.at[1])
    sign = jnp.where(core == 0, 1.0, -1.0).astype(F32)
    dmd = level * (sign * (vel_fold - vel_r[...]))
    dmd_out[...] = jnp.where(core == 0, dmd[:, 0:64], dmd[:, 64:128])
    sca[me_p] = (dmd * LOSS_SCALE).astype(BF16)
    sca_ref = sca.at[me_p]
    to_plane(sca_ref, sca_ref, sca_ssem, sca_rsem)
    got(sca.at[0:15], sca_rsem)

    scaled_rows = sca[...].reshape(512, 128)
    scaled_t = scaled_rows.astype(F32).T.astype(BF16)
    grad_in = jnp.zeros((64, 256), F32)
    grad_out = jnp.zeros((64, 256), F32)
    for h in range(2):
        grad_out = grad_out + mm(scaled_t[h * 64 : h * 64 + 64], hid[h])
        weight = jnp.concatenate([gout_s, zeros] if h == 0 else [zeros, gout_s], axis=0)
        pre = (mm(scaled_rows, weight) * dsil[h]).astype(BF16)
        grad_in = grad_in + mm(noise_t[h * 64 : h * 64 + 64], pre)
    grads = jnp.concatenate([grad_in, grad_out], axis=0)
    lane32 = lanes((32, 128))
    rest = grads[0:32, 128:256]
    for i in range(1, 4):
        rest = jnp.where(lane32 < 32 * i, rest, roll(grads[32 * i : 32 * i + 32, 128:256], 32 * i))
    gpart[0:128, :] = grads[:, 0:128].astype(BF16)
    gpart[128:160, :] = rest.astype(BF16)

    zme = zhi * 4 + zlo
    for k in range(4):

        @pl.when(jnp.logical_not((zhi == core) & (zlo == k)))
        def _(k=k):
            rc(gpart, grecv.at[zme], g_ssem.at[k], g_rsem.at[zme], dev(x, y, core, k, core)).start()

    @pl.when(zhi == core)
    def _():
        total = gpart[...].astype(F32)
        for src in range(8):

            @pl.when(src != zme)
            def _(src=src):
                got(grecv.at[src], g_rsem.at[src])

            @pl.when(src == zme)
            def _(src=src):
                grecv[src] = jnp.zeros((160, 128), BF16)

            total = total + grecv[src].astype(F32)
        fin[32:192, :] = total
        rc(fin.at[32:192], fin.at[32:192], core_ssem.at[2], core_rsem.at[2], partner).start()

    @pl.when(zhi != core)
    def _():
        got(fin.at[32:192], core_rsem.at[2])

    gin_out[:, 0:128] = fin[32:96, :]
    gout_out[:, 0:128] = fin[96:160, :]
    tail = fin[160:192, :]
    for i in range(4):
        ref = gin_out if i < 2 else gout_out
        piece = tail if i == 0 else roll(tail, 128 - 32 * i)
        ref[(i % 2) * 32 : (i % 2) * 32 + 32, 128:160] = piece[:, 0:32]

    for m in range(2):
        for t in range(2):

            @pl.when(jnp.logical_not((zlo == 1 + t) & (core == m)))
            def _(m=m, t=t):
                sent(job_send.at[2 * m + t], job_ssem.at[2 * m + t])

    @pl.when((zlo == 1) | (zlo == 2))
    def _():
        sent(noi.at[0:7], z_ssem)

    for k in range(4):

        @pl.when(jnp.logical_not((zhi == core) & (zlo == k)))
        def _(k=k):
            sent(gpart, g_ssem.at[k])

    @pl.when(zhi == core)
    def _():
        sent(fin.at[32:192], core_ssem.at[2])

    sent(msg, core_ssem.at[0])
    sent(fin.at[0:32], core_ssem.at[1])
    sent(own_ref, tokz_ssem)
    sent(tok.at[0:2, 0:15], tok_ssem)
    sent(ac.at[0:15], ac_ssem)
    sent(noi.at[0:15], noi_ssem)
    sent(sca.at[0:15], sca_ssem)


def body(
    noise_gen,
    noise_add,
    steps_t,
    gen_in,
    gen_out,
    real_in,
    real_qkv,
    real_proj,
    real_head,
    fake_in,
    fake_qkv,
    fake_proj,
    fake_head,
):
    def table(qkv):
        return qkv.transpose(1, 2, 0, 3).reshape(3, 640, 128)

    vmem = pl.BlockSpec(memory_space=pltpu.VMEM)
    hbm = pl.BlockSpec(memory_space=pl.ANY)
    dma = pltpu.SemaphoreType.DMA
    dmd, grad_in, grad_out = pl.pallas_call(
        kernel,
        out_shape=(
            jax.ShapeDtypeStruct((32, 64), F32),
            jax.ShapeDtypeStruct((64, 160), F32),
            jax.ShapeDtypeStruct((64, 160), F32),
        ),
        in_specs=[pl.BlockSpec(memory_space=pltpu.SMEM), vmem, vmem] + [hbm] * 10,
        out_specs=(vmem, vmem, vmem),
        scratch_shapes=[
            pltpu.VMEM((64, 5120), BF16),
            pltpu.VMEM((64, 5120), BF16),
            pltpu.VMEM((64, 5120), BF16),
            pltpu.VMEM((64, 5120), BF16),
            pltpu.VMEM((2, 3, 640, 128), BF16),
            pltpu.VMEM((2, 128, 640), BF16),
            pltpu.VMEM((2, 64, 640), BF16),
            pltpu.VMEM((2, 64, 640), BF16),
            pltpu.VMEM((4, 64, 256), BF16),
            pltpu.VMEM((8, 64, 256), BF16),
            pltpu.VMEM((16, 4, 32, 128), BF16),
            pltpu.VMEM((32, 128), BF16),
            pltpu.VMEM((32, 128), BF16),
            pltpu.VMEM((2, 16, 32, 128), BF16),
            pltpu.VMEM((16, 32, 128), BF16),
            pltpu.VMEM((64, 2048), BF16),
            pltpu.VMEM((2048, 128), BF16),
            pltpu.VMEM((2, 512, 256), BF16),
            pltpu.VMEM((2, 512, 256), F32),
            pltpu.VMEM((64, 64), F32),
            pltpu.VMEM((32, 128), F32),
            pltpu.VMEM((16, 32, 128), BF16),
            pltpu.VMEM((160, 128), BF16),
            pltpu.VMEM((8, 160, 128), BF16),
            pltpu.VMEM((192, 128), F32),
            dma((12,)),
            dma((4,)),
            dma((8,)),
            dma,
            dma((4,)),
            dma,
            dma((16,)),
            dma((3,)),
            dma((3,)),
            dma,
            dma,
            dma,
            dma,
            dma,
            dma,
            dma,
            dma,
            dma((4,)),
            dma((8,)),
        ],
        compiler_params=pltpu.CompilerParams(
            collective_id=0, has_side_effects=True, vmem_limit_bytes=48 * 1024 * 1024
        ),
    )(
        steps_t,
        noise_gen[0],
        noise_add[0],
        gen_in,
        gen_out.T,
        real_in,
        table(real_qkv),
        real_proj[0],
        real_head.T,
        fake_in,
        table(fake_qkv),
        fake_proj[0],
        fake_head.T,
    )
    return dmd[None], grad_in, grad_out.T


def solution(mesh):
    return jax.shard_map(
        body,
        mesh=mesh,
        in_specs=(
            P("mp", "seq", None),
            P("mp", "seq", None),
            P(),
            P(),
            P(),
            P(),
            P("mp", None, "seq", None),
            P("seq", None, "mp"),
            P(),
            P(),
            P("mp", None, "seq", None),
            P("seq", None, "mp"),
            P(),
        ),
        out_specs=(P("mp", "seq", None), P(None, "seq"), P("seq", None)),
        check_vma=False,
    )
```

```python
import functools
import math

import jax
import jax.numpy as jnp
from jax import lax
from jax.experimental import pallas as pl
from jax.experimental.pallas import tpu as pltpu
from jax.sharding import PartitionSpec as P

MESH = pl.DeviceIdType.MESH
F32 = jnp.float32
BF16 = jnp.bfloat16
NN = (((1,), (0,)), ((), ()))
NT = (((1,), (1,)), ((), ()))
HIGH = lax.Precision.HIGHEST
SCORE_SCALE = math.log2(math.e) / math.sqrt(128.0)
LOSS_SCALE = 1.0 / math.sqrt(8192.0)


def mm(a, b, dims=NN, precision=None):
    return lax.dot_general(a, b, dims, precision=precision, preferred_element_type=F32)


def lanes(shape):
    return lax.broadcasted_iota(jnp.int32, shape, len(shape) - 1)


def roll(value, shift):
    return pltpu.roll(value, shift, 1)


def fold(square):
    return jnp.concatenate([square[0:32], square[32:64]], axis=1)


def kernel(
    steps,
    noise_gen,
    noise_add,
    gen_in,
    gen_out,
    real_in,
    real_qkv,
    real_proj,
    real_head,
    fake_in,
    fake_qkv,
    fake_proj,
    fake_head,
    fin,
    steps_s,
    ngen_v,
    nadd_v,
    gin_v,
    gout_v,
    emb_v,
    head_v,
    qkv_v,
    proj_v,
    embs_v,
    heads_v,
    job_send,
    job_recv,
    ac,
    msg,
    msg_r,
    tok,
    noi,
    keys,
    vals_t,
    scores,
    hid,
    dsil,
    vel,
    vel_r,
    sca,
    gpart,
    grecv,
    load_sem,
    job_ssem,
    job_rsem,
    z_ssem,
    z_rsem,
    ac_ssem,
    ac_rsem,
    core_ssem,
    core_rsem,
    tokz_ssem,
    tokz_rsem,
    tok_ssem,
    tok_rsem,
    noi_ssem,
    noi_rsem,
    sca_ssem,
    sca_rsem,
    g_ssem,
    g_rsem,
):
    mp = lax.axis_index("mp")
    seq = lax.axis_index("seq")
    core = mp % 2
    zlo = mp // 2
    x = seq // 8
    zhi = (seq // 4) % 2
    y = seq % 4
    me_p = x * 4 + y

    def dev(x_, y_, zhi_, zlo_, core_):
        return (zlo_ * 2 + core_, x_ * 8 + zhi_ * 4 + y_)

    def plane_dev(k):
        return dev((x + k // 4) % 4, (y + k % 4) % 4, zhi, zlo, core)

    partner = dev(x, y, zhi, zlo, 1 - core)
    across = dev(x, y, 1 - zhi, zlo, core)

    def rc(src, dst, ssem, rsem, device):
        return pltpu.make_async_remote_copy(
            src_ref=src, dst_ref=dst, send_sem=ssem, recv_sem=rsem, device_id=device, device_id_type=MESH
        )

    def to_plane(src, dst, ssem, rsem):
        def send(k, carry):
            rc(src, dst, ssem, rsem, plane_dev(k)).start()
            return carry

        lax.fori_loop(1, 16, send, 0)

    def got(ref, rsem):
        rc(ref, ref, rsem, rsem, partner).wait_recv()

    def sent(ref, ssem):
        rc(ref, ref, ssem, ssem, partner).wait_send()

    row = pl.ds(pl.multiple_of(mp * 640, 128), 640)
    loads = [
        pltpu.make_async_copy(real_in.at[:, row], embs_v.at[0], load_sem.at[0]),
        pltpu.make_async_copy(real_qkv, qkv_v.at[0], load_sem.at[1]),
        pltpu.make_async_copy(real_head.at[:, row], heads_v.at[0], load_sem.at[2]),
        pltpu.make_async_copy(real_proj, proj_v.at[0], load_sem.at[3]),
        pltpu.make_async_copy(fake_in.at[:, row], embs_v.at[1], load_sem.at[4]),
        pltpu.make_async_copy(fake_qkv, qkv_v.at[1], load_sem.at[5]),
        pltpu.make_async_copy(fake_head.at[:, row], heads_v.at[1], load_sem.at[6]),
        pltpu.make_async_copy(fake_proj, proj_v.at[1], load_sem.at[7]),
        pltpu.make_async_copy(gen_in, gin_v, load_sem.at[8]),
        pltpu.make_async_copy(gen_out, gout_v, load_sem.at[9]),
        pltpu.make_async_copy(noise_gen, ngen_v, load_sem.at[12]),
        pltpu.make_async_copy(noise_add, nadd_v, load_sem.at[13]),
        pltpu.make_async_copy(steps, steps_s, load_sem.at[14]),
    ]
    for load in loads:
        load.start()

    @pl.when(core == 0)
    def _():
        pltpu.make_async_copy(real_in, emb_v, load_sem.at[10]).start()
        pltpu.make_async_copy(real_head, head_v, load_sem.at[11]).start()

    @pl.when(core == 1)
    def _():
        pltpu.make_async_copy(fake_in, emb_v, load_sem.at[10]).start()
        pltpu.make_async_copy(fake_head, head_v, load_sem.at[11]).start()

    barrier = pltpu.get_barrier_semaphore()

    def greet(device):
        pl.semaphore_signal(barrier, inc=1, device_id=device, device_id_type=MESH)

    def greet_plane(k, carry):
        greet(plane_dev(k))
        return carry

    def greet_mp(k, carry):
        greet(((mp + k) % 8, seq))
        return carry

    def greet_across(k, carry):
        greet(dev(x, y, 1 - zhi, k, core))
        return carry

    lax.fori_loop(0, 4, greet_across, 0)
    lax.fori_loop(1, 16, greet_plane, 0)
    lax.fori_loop(1, 8, greet_mp, 0)

    for m in range(2):
        for k in range(4):
            loads[4 * m + k].wait()
        for c in range(3):
            job_send[2 * m + c // 2, :, (c % 2) * 128 : (c % 2) * 128 + 128] = mm(embs_v[m], qkv_v[m, c]).astype(BF16)
        job_send[2 * m + 1, :, 128:256] = mm(heads_v[m], proj_v[m], NT).astype(BF16)

    for k in range(8, 13):
        loads[k].wait()
    level = steps_s[zlo].astype(F32) / 1000.0
    own_noise = ngen_v[...]
    clean = own_noise.astype(F32)
    for c in range(5):
        cols = slice(c * 1024, c * 1024 + 1024)
        u = mm(own_noise, gin_v[:, cols])
        hidden = (u * jax.nn.sigmoid(u)).astype(BF16)
        clean = clean + mm(hidden, gout_v[:, cols], NT)
    noised = (1.0 - level) * clean + level * nadd_v[...].astype(F32)
    msg[...] = jnp.concatenate([noised, own_noise.astype(F32)], axis=1).astype(BF16)

    pl.semaphore_wait(barrier, 26)

    for m in range(2):
        for t in range(2):

            @pl.when(jnp.logical_not((zlo == 1 + t) & (core == m)))
            def _(m=m, t=t):
                rc(
                    job_send.at[2 * m + t],
                    job_recv.at[mp],
                    job_ssem.at[2 * m + t],
                    job_rsem.at[mp],
                    dev(x, y, zhi, 1 + t, m),
                ).start()

    rc(msg, msg_r, core_ssem.at[0], core_rsem.at[0], partner).start()
    got(msg_r, core_rsem.at[0])
    left = lanes((32, 128)) < 64
    mine = msg[...].astype(F32)
    other = msg_r[...].astype(F32)
    half0 = jnp.where(core == 0, mine, other)
    half1 = jnp.where(core == 0, other, mine)
    own_tok = jnp.where(left, half0, roll(half1, 64))
    tok[zhi, me_p] = own_tok.astype(BF16)
    noi[me_p] = jnp.where(left, roll(half0, 64), half1).astype(BF16)
    own_ref = tok.at[zhi, me_p]
    rc(own_ref, own_ref, tokz_ssem, tokz_rsem, across).start()
    to_plane(own_ref, own_ref, tok_ssem, tok_rsem)
    xtok = jnp.concatenate([own_tok[:, 0:64], own_tok[:, 64:128]], axis=0)
    xcol = xtok.T.astype(BF16)
    xzero = jnp.zeros((64, 64), BF16)
    xpair = jnp.concatenate(
        [jnp.concatenate([xcol, xzero], axis=1), jnp.concatenate([xzero, xcol], axis=1)], axis=0
    )
    noi_ref = noi.at[me_p]
    to_plane(noi_ref, noi_ref, noi_ssem, noi_rsem)

    pltpu.make_async_copy(real_in, emb_v, load_sem.at[10]).wait()
    pltpu.make_async_copy(real_head, head_v, load_sem.at[11]).wait()
    direct = mm(emb_v[...], head_v[...], NT)
    vel[...] = mm(xtok, direct, precision=HIGH)

    t_here = zlo - 1
    slot_here = zhi * 2 + t_here

    @pl.when((zlo == 1) | (zlo == 2))
    def _():
        total = job_send[core * 2 + t_here].astype(F32)
        for src in range(8):

            @pl.when(src != mp)
            def _(src=src):
                got(job_recv.at[src], job_rsem.at[src])

            @pl.when(src == mp)
            def _(src=src):
                job_recv[src] = jnp.zeros((64, 256), BF16)

            total = total + job_recv[src].astype(F32)
        scale = jnp.where(t_here == 0, SCORE_SCALE, 1.0).astype(F32)
        square = mm(total[:, 128:256], total[:, 0:128], NT, HIGH) * scale
        ac[me_p, slot_here] = fold(square).astype(BF16)
        piece = ac.at[me_p, slot_here]

        def spread(k, carry):
            z = (zhi * 4 + zlo + k) % 8
            rc(piece, piece, z_ssem, z_rsem.at[slot_here], dev(x, y, z // 4, z % 4, core)).start()
            return carry

        lax.fori_loop(1, 8, spread, 0)

    far_ref = tok.at[1 - zhi, me_p]
    got(far_ref, tokz_rsem)
    to_plane(far_ref, far_ref, tok_ssem, tok_rsem)

    upper = zlo // 2
    for order in range(4):
        group = zhi if order < 2 else 1 - zhi
        t = upper if order in (0, 3) else 1 - upper
        slot = group * 2 + t
        piece = ac.at[me_p, slot]

        @pl.when(jnp.logical_not((group == zhi) & (zlo == 1 + t)))
        def _(piece=piece, slot=slot):
            got(piece, z_rsem.at[slot])

        to_plane(piece, piece, ac_ssem, ac_rsem.at[group, me_p])

    got(tok.at[0:2, 0:15], tok_rsem)
    for g in range(2):
        block = tok[g].reshape(512, 128).astype(F32)
        flipped = block.T.astype(BF16)
        rows0 = slice(g * 512, g * 512 + 512)
        rows1 = slice(1024 + g * 512, 1024 + g * 512 + 512)
        vals_t[0:64, rows0] = flipped[0:64]
        vals_t[0:64, rows1] = flipped[64:128]
        keys[rows0, :] = block[:, 0:64].astype(BF16)
        keys[rows1, :] = roll(block, 64)[:, 0:64].astype(BF16)
    vals_t[64:80, :] = jnp.ones((16, 2048), BF16)

    def spots(b):
        return [((x + kx) % 4) * 4 + (y + ky) % 4 for kx in ((0, 1) if b % 2 == 0 else (3, 2)) for ky in range(4)]

    def group_of(b):
        return zhi if b < 2 else 1 - zhi

    def pairs(b, t):
        slot = 2 * group_of(b) + t
        here = spots(b)
        return [(ac[here[i], slot].astype(F32), ac[here[i + 1], slot].astype(F32)) for i in (0, 2, 4, 6)]

    def queries(b):
        for spot in spots(b)[1 if b % 2 == 0 else 0 :]:
            got(ac.at[spot, pl.ds(2 * group_of(b), 2)], ac_rsem.at[group_of(b), spot])
        out = []
        for f0, f1 in pairs(b, 0):
            upper_rows = jnp.where(left, f0, roll(f1, 64))
            lower_rows = jnp.where(left, roll(f0, 64), f1)
            mats = jnp.concatenate([upper_rows, lower_rows], axis=0).astype(BF16)
            out.append(mm(mats, xpair).astype(BF16))
        return jnp.concatenate(out, axis=1)

    def score_chunk(b, q, j, top):
        rows = slice(j * 256, j * 256 + 256)
        s = mm(keys[rows, :], q)
        scores[b % 2, rows, :] = s
        here = jnp.max(s.reshape(32, 8, 512), axis=0)
        return here if top is None else jnp.maximum(top, here)

    def value_chunk(b, top, j, total):
        rows = slice(j * 256, j * 256 + 256)
        weights = jnp.exp2(scores[b % 2, rows, :] - top).astype(BF16)
        part = mm(vals_t[:, rows], weights)
        return part if total is None else total + part

    def finish(b, total, acc):
        mixed = (total[0:64] / total[64:65]).astype(BF16)
        for i, (f0, f1) in enumerate(pairs(b, 1)):
            mats = jnp.concatenate([f0, roll(f0, 64), f1, roll(f1, 64)], axis=0)[:, 0:64].astype(BF16)
            acc = acc + mm(mats, mixed[:, i * 128 : i * 128 + 128])
        return acc

    acc = jnp.zeros((128, 128), F32)
    for b in range(4):
        if b % 2 == 0:
            q = queries(b)
            top = None
            for j in range(8):
                top = score_chunk(b, q, j, top)
        peak = jnp.max(top, axis=0, keepdims=True)
        if b % 2 == 0:
            q = queries(b + 1)
        top = None
        total = None
        for j in range(8):
            if b % 2 == 0:
                top = score_chunk(b + 1, q, j, top)
            total = value_chunk(b, peak, j, total)
        acc = finish(b, total, acc)
    total_vel = vel[...] + (acc[0:64, 0:64] + acc[64:128, 64:128]).T
    vel_fold = jnp.concatenate([total_vel[0:32], total_vel[32:64]], axis=1)
    sca_f = vel_fold
    fin[0:32, :] = sca_f
    rc(fin.at[0:32], vel_r, core_ssem.at[1], core_rsem.at[1], partner).start()

    got(noi.at[0:15], noi_rsem)
    col0 = 160 * (x * 8 + core * 4 + y)
    base = pl.ds(pl.multiple_of((col0 // 128) * 128, 128), 256)
    shift = 256 - 32 * y
    gin_s = pltpu.roll(gin_v[:, base].astype(F32), shift, 1).astype(BF16)
    gout_s = pltpu.roll(gout_v[:, base].astype(F32), shift, 1).astype(BF16)
    zeros = jnp.zeros((64, 256), BF16)
    noise_rows = noi[...].reshape(512, 128)
    for h in range(2):
        weight = jnp.concatenate([gin_s, zeros] if h == 0 else [zeros, gin_s], axis=0)
        u = mm(noise_rows, weight)
        sig = jax.nn.sigmoid(u)
        hid[h] = (u * sig).astype(BF16)
        dsil[h] = sig * (1.0 + u * (1.0 - sig))
    noise_t = noise_rows.astype(F32).T.astype(BF16)

    got(vel_r, core_rsem.at[1])
    sign = jnp.where(core == 0, 1.0, -1.0).astype(F32)
    dmd = level * (sign * (vel_fold - vel_r[...]))
    dmd_full = jnp.where(core == 0, dmd, roll(dmd, 64))
    sca[me_p] = (dmd * LOSS_SCALE).astype(BF16)
    sca_ref = sca.at[me_p]
    to_plane(sca_ref, sca_ref, sca_ssem, sca_rsem)
    got(sca.at[0:15], sca_rsem)

    scaled_rows = sca[...].reshape(512, 128)
    scaled_t = scaled_rows.astype(F32).T.astype(BF16)
    grad_in = jnp.zeros((64, 256), F32)
    grad_out = jnp.zeros((64, 256), F32)
    for h in range(2):
        grad_out = grad_out + mm(scaled_t[h * 64 : h * 64 + 64], hid[h])
        weight = jnp.concatenate([gout_s, zeros] if h == 0 else [zeros, gout_s], axis=0)
        pre = (mm(scaled_rows, weight) * dsil[h]).astype(BF16)
        grad_in = grad_in + mm(noise_t[h * 64 : h * 64 + 64], pre)
    grads = jnp.concatenate([grad_in, grad_out], axis=0)
    lane32 = lanes((32, 128))
    rest = grads[0:32, 128:256]
    for i in range(1, 4):
        rest = jnp.where(lane32 < 32 * i, rest, roll(grads[32 * i : 32 * i + 32, 128:256], 32 * i))
    gpart[0:128, :] = grads[:, 0:128].astype(BF16)
    gpart[128:160, :] = rest.astype(BF16)

    sent(fin.at[0:32], core_ssem.at[1])
    fin[0:32, :] = dmd_full

    zme = zhi * 4 + zlo
    for k in range(4):

        @pl.when(jnp.logical_not((zhi == core) & (zlo == k)))
        def _(k=k):
            rc(gpart, grecv.at[zme], g_ssem.at[k], g_rsem.at[zme], dev(x, y, core, k, core)).start()

    @pl.when(zhi == core)
    def _():
        total = gpart[...].astype(F32)
        for src in range(8):

            @pl.when(src != zme)
            def _(src=src):
                got(grecv.at[src], g_rsem.at[src])

            @pl.when(src == zme)
            def _(src=src):
                grecv[src] = jnp.zeros((160, 128), BF16)

            total = total + grecv[src].astype(F32)
        fin[32:192, :] = total
        rc(fin.at[32:192], fin.at[32:192], core_ssem.at[2], core_rsem.at[2], partner).start()

    @pl.when(zhi != core)
    def _():
        got(fin.at[32:192], core_rsem.at[2])

    for m in range(2):
        for t in range(2):

            @pl.when(jnp.logical_not((zlo == 1 + t) & (core == m)))
            def _(m=m, t=t):
                sent(job_send.at[2 * m + t], job_ssem.at[2 * m + t])

    @pl.when((zlo == 1) | (zlo == 2))
    def _():
        sent(noi.at[0:7], z_ssem)

    for k in range(4):

        @pl.when(jnp.logical_not((zhi == core) & (zlo == k)))
        def _(k=k):
            sent(gpart, g_ssem.at[k])

    @pl.when(zhi == core)
    def _():
        sent(fin.at[32:192], core_ssem.at[2])

    sent(msg, core_ssem.at[0])
    sent(own_ref, tokz_ssem)
    sent(tok.at[0:2, 0:15], tok_ssem)
    sent(ac.at[0:15], ac_ssem)
    sent(noi.at[0:15], noi_ssem)
    sent(sca.at[0:15], sca_ssem)


def unpack(packed, dmd_out, gin_out, gout_out):
    dmd_out[...] = packed[0:32, 0:64]
    gin_out[:, 0:128] = packed[32:96, :]
    gout_out[:, 0:128] = packed[96:160, :]
    tail = packed[160:192, :]
    for i in range(4):
        ref = gin_out if i < 2 else gout_out
        piece = tail if i == 0 else roll(tail, 128 - 32 * i)
        ref[(i % 2) * 32 : (i % 2) * 32 + 32, 128:160] = piece[:, 0:32]


def body(
    noise_gen,
    noise_add,
    steps_t,
    gen_in,
    gen_out,
    real_in,
    real_qkv,
    real_proj,
    real_head,
    fake_in,
    fake_qkv,
    fake_proj,
    fake_head,
):
    def table(qkv):
        return qkv.transpose(1, 2, 0, 3).reshape(3, 640, 128)

    vmem = pl.BlockSpec(memory_space=pltpu.VMEM)
    hbm = pl.BlockSpec(memory_space=pltpu.HBM)
    dma = pltpu.SemaphoreType.DMA
    packed = pl.pallas_call(
        kernel,
        out_shape=jax.ShapeDtypeStruct((192, 128), F32),
        in_specs=[hbm] * 13,
        out_specs=vmem,
        scratch_shapes=[
            pltpu.SMEM((4,), jnp.int32),
            pltpu.VMEM((32, 64), BF16),
            pltpu.VMEM((32, 64), BF16),
            pltpu.VMEM((64, 5120), BF16),
            pltpu.VMEM((64, 5120), BF16),
            pltpu.VMEM((64, 5120), BF16),
            pltpu.VMEM((64, 5120), BF16),
            pltpu.VMEM((2, 3, 640, 128), BF16),
            pltpu.VMEM((2, 128, 640), BF16),
            pltpu.VMEM((2, 64, 640), BF16),
            pltpu.VMEM((2, 64, 640), BF16),
            pltpu.VMEM((4, 64, 256), BF16),
            pltpu.VMEM((8, 64, 256), BF16),
            pltpu.VMEM((16, 4, 32, 128), BF16),
            pltpu.VMEM((32, 128), BF16),
            pltpu.VMEM((32, 128), BF16),
            pltpu.VMEM((2, 16, 32, 128), BF16),
            pltpu.VMEM((16, 32, 128), BF16),
            pltpu.VMEM((2048, 64), BF16),
            pltpu.VMEM((80, 2048), BF16),
            pltpu.VMEM((2, 2048, 512), F32),
            pltpu.VMEM((2, 512, 256), BF16),
            pltpu.VMEM((2, 512, 256), F32),
            pltpu.VMEM((64, 64), F32),
            pltpu.VMEM((32, 128), F32),
            pltpu.VMEM((16, 32, 128), BF16),
            pltpu.VMEM((160, 128), BF16),
            pltpu.VMEM((8, 160, 128), BF16),
            dma((15,)),
            dma((4,)),
            dma((8,)),
            dma,
            dma((4,)),
            dma,
            dma((2, 16)),
            dma((3,)),
            dma((3,)),
            dma,
            dma,
            dma,
            dma,
            dma,
            dma,
            dma,
            dma,
            dma((4,)),
            dma((8,)),
        ],
        compiler_params=pltpu.CompilerParams(
            collective_id=0, has_side_effects=True, vmem_limit_bytes=48 * 1024 * 1024
        ),
    )(
        *(
            pltpu.with_memory_space_constraint(operand, pltpu.HBM)
            for operand in (
                steps_t,
                noise_gen[0],
                noise_add[0],
                gen_in,
                gen_out.T,
                real_in,
                table(real_qkv),
                real_proj[0],
                real_head.T,
                fake_in,
                table(fake_qkv),
                fake_proj[0],
                fake_head.T,
            )
        )
    )
    dmd, grad_in, grad_out = pl.pallas_call(
        unpack,
        out_shape=(
            jax.ShapeDtypeStruct((32, 64), F32),
            jax.ShapeDtypeStruct((64, 160), F32),
            jax.ShapeDtypeStruct((64, 160), F32),
        ),
        in_specs=[vmem],
        out_specs=(vmem, vmem, vmem),
    )(pltpu.with_memory_space_constraint(packed, pltpu.VMEM))
    return dmd[None], grad_in, grad_out.T


def solution(mesh):
    return jax.shard_map(
        body,
        mesh=mesh,
        in_specs=(
            P("mp", "seq", None),
            P("mp", "seq", None),
            P(),
            P(),
            P(),
            P(),
            P("mp", None, "seq", None),
            P("seq", None, "mp"),
            P(),
            P(),
            P("mp", None, "seq", None),
            P("seq", None, "mp"),
            P(),
        ),
        out_specs=(P("mp", "seq", None), P(None, "seq"), P("seq", None)),
        check_vma=False,
    )
```

```python
import functools
import math

import jax
import jax.numpy as jnp
from jax import lax
from jax.experimental import pallas as pl
from jax.experimental.pallas import tpu as pltpu
from jax.sharding import PartitionSpec as P

MESH = pl.DeviceIdType.MESH
F32 = jnp.float32
BF16 = jnp.bfloat16
NN = (((1,), (0,)), ((), ()))
NT = (((1,), (1,)), ((), ()))
HIGH = lax.Precision.HIGHEST
SCORE_SCALE = math.log2(math.e) / math.sqrt(128.0)
LOSS_SCALE = 1.0 / math.sqrt(8192.0)


def mm(a, b, dims=NN, precision=None):
    return lax.dot_general(a, b, dims, precision=precision, preferred_element_type=F32)


def lanes(shape):
    return lax.broadcasted_iota(jnp.int32, shape, len(shape) - 1)


def roll(value, shift):
    return pltpu.roll(value, shift, 1)


def fold(square):
    return jnp.concatenate([square[0:32], square[32:64]], axis=1)


def kernel(
    steps,
    noise_gen,
    noise_add,
    gen_in,
    gen_out,
    real_in,
    real_qkv,
    real_proj,
    real_head,
    fake_in,
    fake_qkv,
    fake_proj,
    fake_head,
    fin,
    steps_s,
    ngen_v,
    nadd_v,
    gin_v,
    gout_v,
    emb_v,
    head_v,
    qkv_v,
    proj_v,
    embs_v,
    heads_v,
    job_send,
    job_recv,
    ac,
    msg,
    msg_r,
    tok,
    noi,
    keys,
    vals_t,
    scores,
    hid,
    dsil,
    vel,
    vel_r,
    sca,
    gpart,
    grecv,
    load_sem,
    job_ssem,
    job_rsem,
    z_ssem,
    z_rsem,
    ac_ssem,
    ac_rsem,
    core_ssem,
    core_rsem,
    tokz_ssem,
    tokz_rsem,
    tok_ssem,
    tok_rsem,
    noi_ssem,
    noi_rsem,
    sca_ssem,
    sca_rsem,
    g_ssem,
    g_rsem,
):
    mp = lax.axis_index("mp")
    seq = lax.axis_index("seq")
    core = mp & 1
    zlo = mp >> 1
    x = seq >> 3
    zhi = (seq >> 2) & 1
    y = seq & 3
    me_p = x * 4 + y

    def dev(x_, y_, zhi_, zlo_, core_):
        return (zlo_ * 2 + core_, x_ * 8 + zhi_ * 4 + y_)

    def gray(v):
        return v ^ (v >> 1)

    def plane_dev(k):
        near = 15 - k
        return dev((x + gray(near >> 2)) & 3, (y + gray(near & 3)) & 3, zhi, zlo, core)

    partner = dev(x, y, zhi, zlo, 1 - core)
    across = dev(x, y, 1 - zhi, zlo, core)

    def rc(src, dst, ssem, rsem, device):
        return pltpu.make_async_remote_copy(
            src_ref=src, dst_ref=dst, send_sem=ssem, recv_sem=rsem, device_id=device, device_id_type=MESH
        )

    def to_plane(src, dst, ssem, rsem):
        def send(k, carry):
            rc(src, dst, ssem, rsem, plane_dev(k)).start()
            return carry

        lax.fori_loop(0, 15, send, 0, unroll=True)

    def got(ref, rsem):
        rc(ref, ref, rsem, rsem, partner).wait_recv()

    def sent(ref, ssem):
        rc(ref, ref, ssem, ssem, partner).wait_send()

    row = pl.ds(pl.multiple_of(mp * 640, 128), 640)
    loads = [
        pltpu.make_async_copy(real_in.at[:, row], embs_v.at[0], load_sem.at[0]),
        pltpu.make_async_copy(real_qkv, qkv_v.at[0], load_sem.at[1]),
        pltpu.make_async_copy(real_head.at[:, row], heads_v.at[0], load_sem.at[2]),
        pltpu.make_async_copy(real_proj, proj_v.at[0], load_sem.at[3]),
        pltpu.make_async_copy(fake_in.at[:, row], embs_v.at[1], load_sem.at[4]),
        pltpu.make_async_copy(fake_qkv, qkv_v.at[1], load_sem.at[5]),
        pltpu.make_async_copy(fake_head.at[:, row], heads_v.at[1], load_sem.at[6]),
        pltpu.make_async_copy(fake_proj, proj_v.at[1], load_sem.at[7]),
        pltpu.make_async_copy(gen_in, gin_v, load_sem.at[8]),
        pltpu.make_async_copy(gen_out, gout_v, load_sem.at[9]),
        pltpu.make_async_copy(noise_gen, ngen_v, load_sem.at[12]),
        pltpu.make_async_copy(noise_add, nadd_v, load_sem.at[13]),
        pltpu.make_async_copy(steps, steps_s, load_sem.at[14]),
    ]
    for load in loads:
        load.start()

    @pl.when(core == 0)
    def _():
        pltpu.make_async_copy(real_in, emb_v, load_sem.at[10]).start()
        pltpu.make_async_copy(real_head, head_v, load_sem.at[11]).start()

    @pl.when(core == 1)
    def _():
        pltpu.make_async_copy(fake_in, emb_v, load_sem.at[10]).start()
        pltpu.make_async_copy(fake_head, head_v, load_sem.at[11]).start()

    barrier = pltpu.get_barrier_semaphore()

    def greet(device):
        pl.semaphore_signal(barrier, inc=1, device_id=device, device_id_type=MESH)

    def greet_plane(k, carry):
        greet(plane_dev(k))
        return carry

    def greet_mp(k, carry):
        greet(((mp + k) & 7, seq))
        return carry

    def greet_across(k, carry):
        greet(dev(x, y, 1 - zhi, k, core))
        return carry

    lax.fori_loop(0, 4, greet_across, 0, unroll=True)
    lax.fori_loop(0, 15, greet_plane, 0, unroll=True)
    lax.fori_loop(1, 8, greet_mp, 0, unroll=True)

    for m in range(2):
        for k in range(4):
            loads[4 * m + k].wait()
        for c in range(3):
            job_send[2 * m + c // 2, :, (c % 2) * 128 : (c % 2) * 128 + 128] = mm(embs_v[m], qkv_v[m, c]).astype(BF16)
        job_send[2 * m + 1, :, 128:256] = mm(heads_v[m], proj_v[m], NT).astype(BF16)

    for k in range(8, 13):
        loads[k].wait()
    level = steps_s[zlo].astype(F32) / 1000.0
    own_noise = ngen_v[...]
    clean = own_noise.astype(F32)
    for c in range(5):
        cols = slice(c * 1024, c * 1024 + 1024)
        u = mm(own_noise, gin_v[:, cols])
        hidden = (u * jax.nn.sigmoid(u)).astype(BF16)
        clean = clean + mm(hidden, gout_v[:, cols], NT)
    noised = (1.0 - level) * clean + level * nadd_v[...].astype(F32)
    msg[...] = jnp.concatenate([noised, own_noise.astype(F32)], axis=1).astype(BF16)

    pl.semaphore_wait(barrier, 26)

    for m in range(2):
        for t in range(2):

            @pl.when(jnp.logical_not((zlo == 1 + t) & (core == m)))
            def _(m=m, t=t):
                rc(
                    job_send.at[2 * m + t],
                    job_recv.at[mp],
                    job_ssem.at[2 * m + t],
                    job_rsem.at[mp],
                    dev(x, y, zhi, 1 + t, m),
                ).start()

    rc(msg, msg_r, core_ssem.at[0], core_rsem.at[0], partner).start()
    got(msg_r, core_rsem.at[0])
    left = lanes((32, 128)) < 64
    mine = msg[...].astype(F32)
    other = msg_r[...].astype(F32)
    half0 = jnp.where(core == 0, mine, other)
    half1 = jnp.where(core == 0, other, mine)
    own_tok = jnp.where(left, half0, roll(half1, 64))
    tok[zhi, me_p] = own_tok.astype(BF16)
    noi[me_p] = jnp.where(left, roll(half0, 64), half1).astype(BF16)
    own_ref = tok.at[zhi, me_p]
    rc(own_ref, own_ref, tokz_ssem, tokz_rsem, across).start()
    to_plane(own_ref, own_ref, tok_ssem, tok_rsem)
    xtok = jnp.concatenate([own_tok[:, 0:64], own_tok[:, 64:128]], axis=0)
    xcol = xtok.T.astype(BF16)
    xzero = jnp.zeros((64, 64), BF16)
    xpair = jnp.concatenate(
        [jnp.concatenate([xcol, xzero], axis=1), jnp.concatenate([xzero, xcol], axis=1)], axis=0
    )
    noi_ref = noi.at[me_p]
    to_plane(noi_ref, noi_ref, noi_ssem, noi_rsem)

    pltpu.make_async_copy(real_in, emb_v, load_sem.at[10]).wait()
    pltpu.make_async_copy(real_head, head_v, load_sem.at[11]).wait()
    direct = mm(emb_v[...], head_v[...], NT)
    vel[...] = mm(xtok, direct, precision=HIGH)

    t_here = zlo - 1
    slot_here = zhi * 2 + t_here

    @pl.when((zlo == 1) | (zlo == 2))
    def _():
        total = job_send[core * 2 + t_here].astype(F32)
        for src in range(8):

            @pl.when(src != mp)
            def _(src=src):
                got(job_recv.at[src], job_rsem.at[src])

            @pl.when(src == mp)
            def _(src=src):
                job_recv[src] = jnp.zeros((64, 256), BF16)

            total = total + job_recv[src].astype(F32)
        scale = jnp.where(t_here == 0, SCORE_SCALE, 1.0).astype(F32)
        square = mm(total[:, 128:256], total[:, 0:128], NT, HIGH) * scale
        ac[me_p, slot_here] = fold(square).astype(BF16)
        piece = ac.at[me_p, slot_here]

        def spread(k, carry):
            z = (zhi * 4 + zlo + k) & 7
            rc(piece, piece, z_ssem, z_rsem.at[slot_here], dev(x, y, z >> 2, z & 3, core)).start()
            return carry

        lax.fori_loop(1, 8, spread, 0, unroll=True)

    far_ref = tok.at[1 - zhi, me_p]
    got(far_ref, tokz_rsem)
    to_plane(far_ref, far_ref, tok_ssem, tok_rsem)

    upper = zlo // 2
    for order in range(4):
        group = zhi if order < 2 else 1 - zhi
        t = upper if order in (0, 3) else 1 - upper
        slot = group * 2 + t
        piece = ac.at[me_p, slot]

        @pl.when(jnp.logical_not((group == zhi) & (zlo == 1 + t)))
        def _(piece=piece, slot=slot):
            got(piece, z_rsem.at[slot])

        to_plane(piece, piece, ac_ssem, ac_rsem.at[group, me_p])

    got(tok.at[0:2, 0:15], tok_rsem)
    for g in range(2):
        block = tok[g].reshape(512, 128).astype(F32)
        flipped = block.T.astype(BF16)
        rows0 = slice(g * 512, g * 512 + 512)
        rows1 = slice(1024 + g * 512, 1024 + g * 512 + 512)
        vals_t[0:64, rows0] = flipped[0:64]
        vals_t[0:64, rows1] = flipped[64:128]
        keys[rows0, :] = block[:, 0:64].astype(BF16)
        keys[rows1, :] = roll(block, 64)[:, 0:64].astype(BF16)
    vals_t[64:80, :] = jnp.ones((16, 2048), BF16)

    near = ((0, 0), (0, 1), (0, 3), (1, 0), (3, 0), (0, 2), (1, 1), (3, 3))
    far = ((1, 3), (3, 1), (2, 0), (1, 2), (3, 2), (2, 1), (2, 3), (2, 2))

    def spots(b):
        return [((x + kx) & 3) * 4 + ((y + ky) & 3) for kx, ky in (near if b % 2 == 0 else far)]

    def group_of(b):
        return zhi if b < 2 else 1 - zhi

    def pairs(b, t):
        slot = 2 * group_of(b) + t
        here = spots(b)
        return [(ac[here[i], slot].astype(F32), ac[here[i + 1], slot].astype(F32)) for i in (0, 2, 4, 6)]

    def queries(b):
        for spot in spots(b)[1 if b % 2 == 0 else 0 :]:
            got(ac.at[spot, pl.ds(2 * group_of(b), 2)], ac_rsem.at[group_of(b), spot])
        out = []
        for f0, f1 in pairs(b, 0):
            upper_rows = jnp.where(left, f0, roll(f1, 64))
            lower_rows = jnp.where(left, roll(f0, 64), f1)
            mats = jnp.concatenate([upper_rows, lower_rows], axis=0).astype(BF16)
            out.append(mm(mats, xpair).astype(BF16))
        return jnp.concatenate(out, axis=1)

    def score_chunk(b, q, j, top):
        rows = slice(j * 256, j * 256 + 256)
        s = mm(keys[rows, :], q)
        scores[b % 2, rows, :] = s
        here = jnp.max(s.reshape(32, 8, 512), axis=0)
        return here if top is None else jnp.maximum(top, here)

    def value_chunk(b, top, j, total):
        rows = slice(j * 256, j * 256 + 256)
        weights = jnp.exp2(scores[b % 2, rows, :] - top).astype(BF16)
        part = mm(vals_t[:, rows], weights)
        return part if total is None else total + part

    def finish(b, total, acc):
        mixed = (total[0:64] / total[64:65]).astype(BF16)
        for i, (f0, f1) in enumerate(pairs(b, 1)):
            mats = jnp.concatenate([f0, roll(f0, 64), f1, roll(f1, 64)], axis=0)[:, 0:64].astype(BF16)
            acc = acc + mm(mats, mixed[:, i * 128 : i * 128 + 128])
        return acc

    acc = jnp.zeros((128, 128), F32)
    for b in range(4):
        if b in (0,):
            q = queries(b)
            top = None
            for j in range(8):
                top = score_chunk(b, q, j, top)
        peak = jnp.max(top, axis=0, keepdims=True)
        if b in (0, 1, 2):
            q = queries(b + 1)
        top = None
        total = None
        for j in range(8):
            if b in (0, 1, 2):
                top = score_chunk(b + 1, q, j, top)
            total = value_chunk(b, peak, j, total)
        acc = finish(b, total, acc)
    total_vel = vel[...] + (acc[0:64, 0:64] + acc[64:128, 64:128]).T
    vel_fold = jnp.concatenate([total_vel[0:32], total_vel[32:64]], axis=1)
    sca_f = vel_fold
    fin[0:32, :] = sca_f
    rc(fin.at[0:32], vel_r, core_ssem.at[1], core_rsem.at[1], partner).start()

    got(noi.at[0:15], noi_rsem)
    col0 = 160 * (x * 8 + core * 4 + y)
    base = pl.ds(pl.multiple_of((col0 // 128) * 128, 128), 256)
    shift = 256 - 32 * y
    gin_s = pltpu.roll(gin_v[:, base].astype(F32), shift, 1).astype(BF16)
    gout_s = pltpu.roll(gout_v[:, base].astype(F32), shift, 1).astype(BF16)
    zeros = jnp.zeros((64, 256), BF16)
    noise_rows = noi[...].reshape(512, 128)
    for h in range(2):
        weight = jnp.concatenate([gin_s, zeros] if h == 0 else [zeros, gin_s], axis=0)
        u = mm(noise_rows, weight)
        sig = jax.nn.sigmoid(u)
        hid[h] = (u * sig).astype(BF16)
        dsil[h] = sig * (1.0 + u * (1.0 - sig))
    noise_t = noise_rows.astype(F32).T.astype(BF16)

    got(vel_r, core_rsem.at[1])
    sign = jnp.where(core == 0, 1.0, -1.0).astype(F32)
    dmd = level * (sign * (vel_fold - vel_r[...]))
    dmd_full = jnp.where(core == 0, dmd, roll(dmd, 64))
    sca[me_p] = (dmd * LOSS_SCALE).astype(BF16)
    sca_ref = sca.at[me_p]
    to_plane(sca_ref, sca_ref, sca_ssem, sca_rsem)
    got(sca.at[0:15], sca_rsem)

    scaled_rows = sca[...].reshape(512, 128)
    scaled_t = scaled_rows.astype(F32).T.astype(BF16)
    grad_in = jnp.zeros((64, 256), F32)
    grad_out = jnp.zeros((64, 256), F32)
    for h in range(2):
        grad_out = grad_out + mm(scaled_t[h * 64 : h * 64 + 64], hid[h])
        weight = jnp.concatenate([gout_s, zeros] if h == 0 else [zeros, gout_s], axis=0)
        pre = (mm(scaled_rows, weight) * dsil[h]).astype(BF16)
        grad_in = grad_in + mm(noise_t[h * 64 : h * 64 + 64], pre)
    grads = jnp.concatenate([grad_in, grad_out], axis=0)
    lane32 = lanes((32, 128))
    rest = grads[0:32, 128:256]
    for i in range(1, 4):
        rest = jnp.where(lane32 < 32 * i, rest, roll(grads[32 * i : 32 * i + 32, 128:256], 32 * i))
    gpart[0:128, :] = grads[:, 0:128].astype(BF16)
    gpart[128:160, :] = rest.astype(BF16)

    sent(fin.at[0:32], core_ssem.at[1])
    fin[0:32, :] = dmd_full

    zme = zhi * 4 + zlo
    for k in range(4):

        @pl.when(jnp.logical_not((zhi == core) & (zlo == k)))
        def _(k=k):
            rc(gpart, grecv.at[zme], g_ssem.at[k], g_rsem.at[zme], dev(x, y, core, k, core)).start()

    @pl.when(zhi == core)
    def _():
        total = gpart[...].astype(F32)
        for src in range(8):

            @pl.when(src != zme)
            def _(src=src):
                got(grecv.at[src], g_rsem.at[src])

            @pl.when(src == zme)
            def _(src=src):
                grecv[src] = jnp.zeros((160, 128), BF16)

            total = total + grecv[src].astype(F32)
        fin[32:192, :] = total
        rc(fin.at[32:192], fin.at[32:192], core_ssem.at[2], core_rsem.at[2], partner).start()

    @pl.when(zhi != core)
    def _():
        got(fin.at[32:192], core_rsem.at[2])

    for m in range(2):
        for t in range(2):

            @pl.when(jnp.logical_not((zlo == 1 + t) & (core == m)))
            def _(m=m, t=t):
                sent(job_send.at[2 * m + t], job_ssem.at[2 * m + t])

    @pl.when((zlo == 1) | (zlo == 2))
    def _():
        sent(noi.at[0:7], z_ssem)

    for k in range(4):

        @pl.when(jnp.logical_not((zhi == core) & (zlo == k)))
        def _(k=k):
            sent(gpart, g_ssem.at[k])

    @pl.when(zhi == core)
    def _():
        sent(fin.at[32:192], core_ssem.at[2])

    sent(msg, core_ssem.at[0])
    sent(own_ref, tokz_ssem)
    sent(tok.at[0:2, 0:15], tok_ssem)
    sent(ac.at[0:15], ac_ssem)
    sent(noi.at[0:15], noi_ssem)
    sent(sca.at[0:15], sca_ssem)


def unpack(packed, dmd_out, gin_out, gout_out):
    dmd_out[...] = packed[0:32, 0:64]
    gin_out[:, 0:128] = packed[32:96, :]
    gout_out[:, 0:128] = packed[96:160, :]
    tail = packed[160:192, :]
    for i in range(4):
        ref = gin_out if i < 2 else gout_out
        piece = tail if i == 0 else roll(tail, 128 - 32 * i)
        ref[(i % 2) * 32 : (i % 2) * 32 + 32, 128:160] = piece[:, 0:32]


def body(
    noise_gen,
    noise_add,
    steps_t,
    gen_in,
    gen_out,
    real_in,
    real_qkv,
    real_proj,
    real_head,
    fake_in,
    fake_qkv,
    fake_proj,
    fake_head,
):
    def table(qkv):
        return qkv.transpose(1, 2, 0, 3).reshape(3, 640, 128)

    vmem = pl.BlockSpec(memory_space=pltpu.VMEM)
    hbm = pl.BlockSpec(memory_space=pltpu.HBM)
    dma = pltpu.SemaphoreType.DMA
    packed = pl.pallas_call(
        kernel,
        out_shape=jax.ShapeDtypeStruct((192, 128), F32),
        in_specs=[hbm] * 13,
        out_specs=vmem,
        scratch_shapes=[
            pltpu.SMEM((4,), jnp.int32),
            pltpu.VMEM((32, 64), BF16),
            pltpu.VMEM((32, 64), BF16),
            pltpu.VMEM((64, 5120), BF16),
            pltpu.VMEM((64, 5120), BF16),
            pltpu.VMEM((64, 5120), BF16),
            pltpu.VMEM((64, 5120), BF16),
            pltpu.VMEM((2, 3, 640, 128), BF16),
            pltpu.VMEM((2, 128, 640), BF16),
            pltpu.VMEM((2, 64, 640), BF16),
            pltpu.VMEM((2, 64, 640), BF16),
            pltpu.VMEM((4, 64, 256), BF16),
            pltpu.VMEM((8, 64, 256), BF16),
            pltpu.VMEM((16, 4, 32, 128), BF16),
            pltpu.VMEM((32, 128), BF16),
            pltpu.VMEM((32, 128), BF16),
            pltpu.VMEM((2, 16, 32, 128), BF16),
            pltpu.VMEM((16, 32, 128), BF16),
            pltpu.VMEM((2048, 64), BF16),
            pltpu.VMEM((80, 2048), BF16),
            pltpu.VMEM((2, 2048, 512), F32),
            pltpu.VMEM((2, 512, 256), BF16),
            pltpu.VMEM((2, 512, 256), F32),
            pltpu.VMEM((64, 64), F32),
            pltpu.VMEM((32, 128), F32),
            pltpu.VMEM((16, 32, 128), BF16),
            pltpu.VMEM((160, 128), BF16),
            pltpu.VMEM((8, 160, 128), BF16),
            dma((15,)),
            dma((4,)),
            dma((8,)),
            dma,
            dma((4,)),
            dma,
            dma((2, 16)),
            dma((3,)),
            dma((3,)),
            dma,
            dma,
            dma,
            dma,
            dma,
            dma,
            dma,
            dma,
            dma((4,)),
            dma((8,)),
        ],
        compiler_params=pltpu.CompilerParams(
            collective_id=0, has_side_effects=True, vmem_limit_bytes=48 * 1024 * 1024
        ),
    )(
        *(
            pltpu.with_memory_space_constraint(operand, pltpu.HBM)
            for operand in (
                steps_t,
                noise_gen[0],
                noise_add[0],
                gen_in,
                gen_out.T,
                real_in,
                table(real_qkv),
                real_proj[0],
                real_head.T,
                fake_in,
                table(fake_qkv),
                fake_proj[0],
                fake_head.T,
            )
        )
    )
    dmd, grad_in, grad_out = pl.pallas_call(
        unpack,
        out_shape=(
            jax.ShapeDtypeStruct((32, 64), F32),
            jax.ShapeDtypeStruct((64, 160), F32),
            jax.ShapeDtypeStruct((64, 160), F32),
        ),
        in_specs=[vmem],
        out_specs=(vmem, vmem, vmem),
    )(pltpu.with_memory_space_constraint(packed, pltpu.VMEM))
    return dmd[None], grad_in, grad_out.T


def solution(mesh):
    return jax.shard_map(
        body,
        mesh=mesh,
        in_specs=(
            P("mp", "seq", None),
            P("mp", "seq", None),
            P(),
            P(),
            P(),
            P(),
            P("mp", None, "seq", None),
            P("seq", None, "mp"),
            P(),
            P(),
            P("mp", None, "seq", None),
            P("seq", None, "mp"),
            P(),
        ),
        out_specs=(P("mp", "seq", None), P(None, "seq"), P("seq", None)),
        check_vma=False,
    )
```

```python
import functools
import math

import jax
import jax.numpy as jnp
from jax import lax
from jax.experimental import pallas as pl
from jax.experimental.pallas import tpu as pltpu
from jax.sharding import PartitionSpec as P

MESH = pl.DeviceIdType.MESH
F32 = jnp.float32
BF16 = jnp.bfloat16
NN = (((1,), (0,)), ((), ()))
NT = (((1,), (1,)), ((), ()))
HIGH = lax.Precision.HIGHEST
SCORE_SCALE = math.log2(math.e) / math.sqrt(128.0)
LOSS_SCALE = 1.0 / math.sqrt(8192.0)


def mm(a, b, dims=NN, precision=None):
    return lax.dot_general(a, b, dims, precision=precision, preferred_element_type=F32)


def lanes(shape):
    return lax.broadcasted_iota(jnp.int32, shape, len(shape) - 1)


def roll(value, shift):
    return pltpu.roll(value, shift, 1)


def fold(square):
    return jnp.concatenate([square[0:32], square[32:64]], axis=1)


def kernel(
    steps,
    noise_gen,
    noise_add,
    gen_in,
    gen_out,
    real_in,
    real_qkv,
    real_proj,
    real_head,
    fake_in,
    fake_qkv,
    fake_proj,
    fake_head,
    fin,
    steps_s,
    ngen_v,
    nadd_v,
    gin_v,
    gout_v,
    emb_v,
    head_v,
    qkv_v,
    proj_v,
    embs_v,
    heads_v,
    job_send,
    job_recv,
    ac,
    msg,
    msg_r,
    tok,
    noi,
    keys,
    vals_t,
    scores,
    hid,
    dsil,
    vel,
    vel_r,
    sca,
    gpart,
    grecv,
    load_sem,
    job_ssem,
    job_rsem,
    z_ssem,
    z_rsem,
    ac_ssem,
    ac_rsem,
    core_ssem,
    core_rsem,
    tokz_ssem,
    tokz_rsem,
    tok_ssem,
    tok_rsem,
    noi_ssem,
    noi_rsem,
    sca_ssem,
    sca_rsem,
    g_ssem,
    g_rsem,
):
    mp = lax.axis_index("mp")
    seq = lax.axis_index("seq")
    core = mp & 1
    zlo = mp >> 1
    x = seq >> 3
    zhi = (seq >> 2) & 1
    y = seq & 3
    me_p = x * 4 + y

    def dev(x_, y_, zhi_, zlo_, core_):
        return (zlo_ * 2 + core_, x_ * 8 + zhi_ * 4 + y_)

    def gray(v):
        return v ^ (v >> 1)

    def plane_dev(k):
        near = 15 - k
        return dev((x + gray(near >> 2)) & 3, (y + gray(near & 3)) & 3, zhi, zlo, core)

    partner = dev(x, y, zhi, zlo, 1 - core)
    across = dev(x, y, 1 - zhi, zlo, core)

    def rc(src, dst, ssem, rsem, device):
        return pltpu.make_async_remote_copy(
            src_ref=src, dst_ref=dst, send_sem=ssem, recv_sem=rsem, device_id=device, device_id_type=MESH
        )

    def to_plane(src, dst, ssem, rsem):
        def send(k, carry):
            rc(src, dst, ssem, rsem, plane_dev(k)).start()
            return carry

        lax.fori_loop(0, 15, send, 0, unroll=True)

    def got(ref, rsem):
        rc(ref, ref, rsem, rsem, partner).wait_recv()

    def sent(ref, ssem):
        rc(ref, ref, ssem, ssem, partner).wait_send()

    row = pl.ds(pl.multiple_of(mp * 640, 128), 640)
    loads = [
        pltpu.make_async_copy(real_in.at[:, row], embs_v.at[0], load_sem.at[0]),
        pltpu.make_async_copy(real_qkv, qkv_v.at[0], load_sem.at[1]),
        pltpu.make_async_copy(real_head.at[:, row], heads_v.at[0], load_sem.at[2]),
        pltpu.make_async_copy(real_proj, proj_v.at[0], load_sem.at[3]),
        pltpu.make_async_copy(fake_in.at[:, row], embs_v.at[1], load_sem.at[4]),
        pltpu.make_async_copy(fake_qkv, qkv_v.at[1], load_sem.at[5]),
        pltpu.make_async_copy(fake_head.at[:, row], heads_v.at[1], load_sem.at[6]),
        pltpu.make_async_copy(fake_proj, proj_v.at[1], load_sem.at[7]),
        pltpu.make_async_copy(gen_in, gin_v, load_sem.at[8]),
        pltpu.make_async_copy(gen_out, gout_v, load_sem.at[9]),
        pltpu.make_async_copy(noise_gen, ngen_v, load_sem.at[12]),
        pltpu.make_async_copy(noise_add, nadd_v, load_sem.at[13]),
        pltpu.make_async_copy(steps, steps_s, load_sem.at[14]),
    ]
    for load in loads:
        load.start()

    @pl.when(core == 0)
    def _():
        pltpu.make_async_copy(real_in, emb_v, load_sem.at[10]).start()
        pltpu.make_async_copy(real_head, head_v, load_sem.at[11]).start()

    @pl.when(core == 1)
    def _():
        pltpu.make_async_copy(fake_in, emb_v, load_sem.at[10]).start()
        pltpu.make_async_copy(fake_head, head_v, load_sem.at[11]).start()

    barrier = pltpu.get_barrier_semaphore()

    def greet(device):
        pl.semaphore_signal(barrier, inc=1, device_id=device, device_id_type=MESH)

    def greet_plane(k, carry):
        greet(plane_dev(k))
        return carry

    def greet_mp(k, carry):
        greet(((mp + k) & 7, seq))
        return carry

    def greet_across(k, carry):
        greet(dev(x, y, 1 - zhi, k, core))
        return carry

    lax.fori_loop(0, 4, greet_across, 0, unroll=True)
    lax.fori_loop(0, 15, greet_plane, 0, unroll=True)
    lax.fori_loop(1, 8, greet_mp, 0, unroll=True)

    for m in range(2):
        for k in range(4):
            loads[4 * m + k].wait()
        for c in range(3):
            job_send[2 * m + c // 2, :, (c % 2) * 128 : (c % 2) * 128 + 128] = mm(embs_v[m], qkv_v[m, c]).astype(BF16)
        job_send[2 * m + 1, :, 128:256] = mm(heads_v[m], proj_v[m], NT).astype(BF16)

    for k in range(8, 13):
        loads[k].wait()
    level = steps_s[zlo].astype(F32) / 1000.0
    own_noise = ngen_v[...]
    clean = own_noise.astype(F32)
    for c in range(5):
        cols = slice(c * 1024, c * 1024 + 1024)
        u = mm(own_noise, gin_v[:, cols])
        hidden = (u * jax.nn.sigmoid(u)).astype(BF16)
        clean = clean + mm(hidden, gout_v[:, cols], NT)
    noised = (1.0 - level) * clean + level * nadd_v[...].astype(F32)
    msg[...] = jnp.concatenate([noised, own_noise.astype(F32)], axis=1).astype(BF16)

    pl.semaphore_wait(barrier, 26)

    for m in range(2):
        for t in range(2):

            @pl.when(jnp.logical_not((zlo == 1 + t) & (core == m)))
            def _(m=m, t=t):
                rc(
                    job_send.at[2 * m + t],
                    job_recv.at[mp],
                    job_ssem.at[2 * m + t],
                    job_rsem.at[mp],
                    dev(x, y, zhi, 1 + t, m),
                ).start()

    rc(msg, msg_r, core_ssem.at[0], core_rsem.at[0], partner).start()
    got(msg_r, core_rsem.at[0])
    left = lanes((32, 128)) < 64
    mine = msg[...].astype(F32)
    other = msg_r[...].astype(F32)
    half0 = jnp.where(core == 0, mine, other)
    half1 = jnp.where(core == 0, other, mine)
    own_tok = jnp.where(left, half0, roll(half1, 64))
    tok[zhi, me_p] = own_tok.astype(BF16)
    noi[me_p] = jnp.where(left, roll(half0, 64), half1).astype(BF16)
    own_ref = tok.at[zhi, me_p]
    rc(own_ref, own_ref, tokz_ssem, tokz_rsem, across).start()
    to_plane(own_ref, own_ref, tok_ssem, tok_rsem)
    xtok = jnp.concatenate([own_tok[:, 0:64], own_tok[:, 64:128]], axis=0)
    xcol = xtok.T.astype(BF16)
    xzero = jnp.zeros((64, 64), BF16)
    xpair = jnp.concatenate(
        [jnp.concatenate([xcol, xzero], axis=1), jnp.concatenate([xzero, xcol], axis=1)], axis=0
    )
    noi_ref = noi.at[me_p]
    to_plane(noi_ref, noi_ref, noi_ssem, noi_rsem)

    pltpu.make_async_copy(real_in, emb_v, load_sem.at[10]).wait()
    pltpu.make_async_copy(real_head, head_v, load_sem.at[11]).wait()
    direct = mm(emb_v[...], head_v[...], NT)
    vel[...] = mm(xtok, direct, precision=HIGH)

    t_here = zlo - 1
    slot_here = zhi * 2 + t_here

    @pl.when((zlo == 1) | (zlo == 2))
    def _():
        total = job_send[core * 2 + t_here].astype(F32)
        for src in range(8):

            @pl.when(src != mp)
            def _(src=src):
                got(job_recv.at[src], job_rsem.at[src])

            @pl.when(src == mp)
            def _(src=src):
                job_recv[src] = jnp.zeros((64, 256), BF16)

            total = total + job_recv[src].astype(F32)
        scale = jnp.where(t_here == 0, SCORE_SCALE, 1.0).astype(F32)
        square = mm(total[:, 128:256], total[:, 0:128], NT, HIGH) * scale
        ac[me_p, slot_here] = fold(square).astype(BF16)
        piece = ac.at[me_p, slot_here]

        def spread(k, carry):
            z = (zhi * 4 + zlo + k) & 7
            rc(piece, piece, z_ssem, z_rsem.at[slot_here], dev(x, y, z >> 2, z & 3, core)).start()
            return carry

        lax.fori_loop(1, 8, spread, 0, unroll=True)

    far_ref = tok.at[1 - zhi, me_p]
    got(far_ref, tokz_rsem)
    to_plane(far_ref, far_ref, tok_ssem, tok_rsem)

    upper = zlo // 2
    for order in range(4):
        group = zhi if order < 2 else 1 - zhi
        t = upper if order in (0, 3) else 1 - upper
        slot = group * 2 + t
        piece = ac.at[me_p, slot]

        @pl.when(jnp.logical_not((group == zhi) & (zlo == 1 + t)))
        def _(piece=piece, slot=slot):
            got(piece, z_rsem.at[slot])

        to_plane(piece, piece, ac_ssem, ac_rsem.at[group, me_p])

    got(tok.at[0:2, 0:15], tok_rsem)
    for g in range(2):
        block = tok[g].reshape(512, 128).astype(F32)
        flipped = block.T.astype(BF16)
        rows0 = slice(g * 512, g * 512 + 512)
        rows1 = slice(1024 + g * 512, 1024 + g * 512 + 512)
        vals_t[0:64, rows0] = flipped[0:64]
        vals_t[0:64, rows1] = flipped[64:128]
        keys[rows0, :] = block[:, 0:64].astype(BF16)
        keys[rows1, :] = roll(block, 64)[:, 0:64].astype(BF16)
    vals_t[64:80, :] = jnp.ones((16, 2048), BF16)

    near = ((0, 0), (0, 1), (0, 3), (1, 0), (3, 0), (0, 2), (1, 1), (3, 3))
    far = ((1, 3), (3, 1), (2, 0), (1, 2), (3, 2), (2, 1), (2, 3), (2, 2))

    def spots(b):
        return [((x + kx) & 3) * 4 + ((y + ky) & 3) for kx, ky in (near if b % 2 == 0 else far)]

    def group_of(b):
        return zhi if b < 2 else 1 - zhi

    def pairs(b, t):
        slot = 2 * group_of(b) + t
        here = spots(b)
        return [(ac[here[i], slot].astype(F32), ac[here[i + 1], slot].astype(F32)) for i in (0, 2, 4, 6)]

    def queries(b):
        for spot in spots(b)[1 if b % 2 == 0 else 0 :]:
            got(ac.at[spot, pl.ds(2 * group_of(b), 2)], ac_rsem.at[group_of(b), spot])
        out = []
        for f0, f1 in pairs(b, 0):
            upper_rows = jnp.where(left, f0, roll(f1, 64))
            lower_rows = jnp.where(left, roll(f0, 64), f1)
            mats = jnp.concatenate([upper_rows, lower_rows], axis=0).astype(BF16)
            out.append(mm(mats, xpair).astype(BF16))
        return jnp.concatenate(out, axis=1)

    def score_chunk(b, q, j, top):
        rows = slice(j * 256, j * 256 + 256)
        s = mm(keys[rows, :], q)
        scores[b % 2, rows, :] = s
        here = jnp.max(s.reshape(32, 8, 512), axis=0)
        return here if top is None else jnp.maximum(top, here)

    def value_chunk(b, top, j, total):
        rows = slice(j * 256, j * 256 + 256)
        weights = jnp.exp2(scores[b % 2, rows, :] - top).astype(BF16)
        part = mm(vals_t[:, rows], weights)
        return part if total is None else total + part

    def finish(b, total, acc):
        mixed = (total[0:64] / total[64:65]).astype(BF16)
        for i, (f0, f1) in enumerate(pairs(b, 1)):
            mats = jnp.concatenate([f0, roll(f0, 64), f1, roll(f1, 64)], axis=0)[:, 0:64].astype(BF16)
            acc = acc + mm(mats, mixed[:, i * 128 : i * 128 + 128])
        return acc

    acc = jnp.zeros((128, 128), F32)
    for b in range(4):
        if b in (0,):
            q = queries(b)
            top = None
            for j in range(8):
                top = score_chunk(b, q, j, top)
        peak = jnp.max(top, axis=0, keepdims=True)
        if b in (0, 1, 2):
            q = queries(b + 1)
        top = None
        total = None
        for j in range(8):
            if b in (0, 1, 2):
                top = score_chunk(b + 1, q, j, top)
            total = value_chunk(b, peak, j, total)
        acc = finish(b, total, acc)
    total_vel = vel[...] + (acc[0:64, 0:64] + acc[64:128, 64:128]).T
    vel_fold = jnp.concatenate([total_vel[0:32], total_vel[32:64]], axis=1)
    sca_f = vel_fold
    fin[0:32, :] = sca_f
    rc(fin.at[0:32], vel_r, core_ssem.at[1], core_rsem.at[1], partner).start()

    got(noi.at[0:15], noi_rsem)
    col0 = 160 * (x * 8 + core * 4 + y)
    base = pl.ds(pl.multiple_of((col0 // 128) * 128, 128), 256)
    shift = 256 - 32 * y
    gin_s = pltpu.roll(gin_v[:, base].astype(F32), shift, 1).astype(BF16)
    gout_s = pltpu.roll(gout_v[:, base].astype(F32), shift, 1).astype(BF16)
    zeros = jnp.zeros((64, 256), BF16)
    noise_rows = noi[...].reshape(512, 128)
    for h in range(2):
        weight = jnp.concatenate([gin_s, zeros] if h == 0 else [zeros, gin_s], axis=0)
        u = mm(noise_rows, weight)
        sig = jax.nn.sigmoid(u)
        hid[h] = (u * sig).astype(BF16)
        dsil[h] = sig * (1.0 + u * (1.0 - sig))
    noise_t = noise_rows.astype(F32).T.astype(BF16)

    got(vel_r, core_rsem.at[1])
    sign = jnp.where(core == 0, 1.0, -1.0).astype(F32)
    dmd = level * (sign * (vel_fold - vel_r[...]))
    dmd_full = jnp.where(core == 0, dmd, roll(dmd, 64))
    sca[me_p] = (dmd * LOSS_SCALE).astype(BF16)
    sca_ref = sca.at[me_p]
    to_plane(sca_ref, sca_ref, sca_ssem, sca_rsem)
    got(sca.at[0:15], sca_rsem)

    scaled_rows = sca[...].reshape(512, 128)
    scaled_t = scaled_rows.astype(F32).T.astype(BF16)
    zme = zhi * 4 + zlo

    def to_owners(part, grads):
        lane32 = lanes((16, 128))
        rest = grads[0:16, 128:256]
        for i in range(1, 4):
            rest = jnp.where(lane32 < 32 * i, rest, roll(grads[16 * i : 16 * i + 16, 128:256], 32 * i))
        gpart[part, 0:64, :] = grads[:, 0:128].astype(BF16)
        gpart[part, 64:80, :] = rest.astype(BF16)
        for k in range(4):

            @pl.when(jnp.logical_not((zhi == core) & (zlo == k)))
            def _(k=k):
                rc(
                    gpart.at[part],
                    grecv.at[zme, part],
                    g_ssem.at[part, k],
                    g_rsem.at[part, zme],
                    dev(x, y, core, k, core),
                ).start()

    grad_out = mm(scaled_t[0:64], hid[0]) + mm(scaled_t[64:128], hid[1])
    to_owners(1, grad_out)
    grad_in = jnp.zeros((64, 256), F32)
    for h in range(2):
        weight = jnp.concatenate([gout_s, zeros] if h == 0 else [zeros, gout_s], axis=0)
        pre = (mm(scaled_rows, weight) * dsil[h]).astype(BF16)
        grad_in = grad_in + mm(noise_t[h * 64 : h * 64 + 64], pre)
    to_owners(0, grad_in)
    sent(fin.at[0:32], core_ssem.at[1])
    fin[0:32, :] = dmd_full

    @pl.when(zhi == core)
    def _():
        for part in (1, 0):
            total = gpart[part].astype(F32)
            for src in range(8):

                @pl.when(src != zme)
                def _(src=src, part=part):
                    got(grecv.at[src, part], g_rsem.at[part, src])

                @pl.when(src == zme)
                def _(src=src, part=part):
                    grecv[src, part] = jnp.zeros((80, 128), BF16)

                total = total + grecv[src, part].astype(F32)
            fin[32 + 80 * part : 112 + 80 * part, :] = total
        rc(fin.at[32:192], fin.at[32:192], core_ssem.at[2], core_rsem.at[2], partner).start()

    @pl.when(zhi != core)
    def _():
        got(fin.at[32:192], core_rsem.at[2])

    for m in range(2):
        for t in range(2):

            @pl.when(jnp.logical_not((zlo == 1 + t) & (core == m)))
            def _(m=m, t=t):
                sent(job_send.at[2 * m + t], job_ssem.at[2 * m + t])

    @pl.when((zlo == 1) | (zlo == 2))
    def _():
        sent(noi.at[0:7], z_ssem)

    for k in range(4):

        @pl.when(jnp.logical_not((zhi == core) & (zlo == k)))
        def _(k=k):
            sent(gpart.at[0], g_ssem.at[0, k])
            sent(gpart.at[1], g_ssem.at[1, k])

    @pl.when(zhi == core)
    def _():
        sent(fin.at[32:192], core_ssem.at[2])

    sent(msg, core_ssem.at[0])
    sent(own_ref, tokz_ssem)
    sent(tok.at[0:2, 0:15], tok_ssem)
    sent(ac.at[0:15], ac_ssem)
    sent(noi.at[0:15], noi_ssem)
    sent(sca.at[0:15], sca_ssem)


def unpack(packed, dmd_out, gin_out, gout_out):
    dmd_out[...] = packed[0:32, 0:64]
    for ref, at in ((gin_out, 32), (gout_out, 112)):
        ref[:, 0:128] = packed[at : at + 64, :]
        tail = packed[at + 64 : at + 80, :]
        for i in range(4):
            piece = tail if i == 0 else roll(tail, 128 - 32 * i)
            ref[16 * i : 16 * i + 16, 128:160] = piece[:, 0:32]


def body(
    noise_gen,
    noise_add,
    steps_t,
    gen_in,
    gen_out,
    real_in,
    real_qkv,
    real_proj,
    real_head,
    fake_in,
    fake_qkv,
    fake_proj,
    fake_head,
):
    def table(qkv):
        return qkv.transpose(1, 2, 0, 3).reshape(3, 640, 128)

    vmem = pl.BlockSpec(memory_space=pltpu.VMEM)
    hbm = pl.BlockSpec(memory_space=pltpu.HBM)
    dma = pltpu.SemaphoreType.DMA
    packed = pl.pallas_call(
        kernel,
        out_shape=jax.ShapeDtypeStruct((192, 128), F32),
        in_specs=[hbm] * 13,
        out_specs=vmem,
        scratch_shapes=[
            pltpu.SMEM((4,), jnp.int32),
            pltpu.VMEM((32, 64), BF16),
            pltpu.VMEM((32, 64), BF16),
            pltpu.VMEM((64, 5120), BF16),
            pltpu.VMEM((64, 5120), BF16),
            pltpu.VMEM((64, 5120), BF16),
            pltpu.VMEM((64, 5120), BF16),
            pltpu.VMEM((2, 3, 640, 128), BF16),
            pltpu.VMEM((2, 128, 640), BF16),
            pltpu.VMEM((2, 64, 640), BF16),
            pltpu.VMEM((2, 64, 640), BF16),
            pltpu.VMEM((4, 64, 256), BF16),
            pltpu.VMEM((8, 64, 256), BF16),
            pltpu.VMEM((16, 4, 32, 128), BF16),
            pltpu.VMEM((32, 128), BF16),
            pltpu.VMEM((32, 128), BF16),
            pltpu.VMEM((2, 16, 32, 128), BF16),
            pltpu.VMEM((16, 32, 128), BF16),
            pltpu.VMEM((2048, 64), BF16),
            pltpu.VMEM((80, 2048), BF16),
            pltpu.VMEM((2, 2048, 512), F32),
            pltpu.VMEM((2, 512, 256), BF16),
            pltpu.VMEM((2, 512, 256), F32),
            pltpu.VMEM((64, 64), F32),
            pltpu.VMEM((32, 128), F32),
            pltpu.VMEM((16, 32, 128), BF16),
            pltpu.VMEM((2, 80, 128), BF16),
            pltpu.VMEM((8, 2, 80, 128), BF16),
            dma((15,)),
            dma((4,)),
            dma((8,)),
            dma,
            dma((4,)),
            dma,
            dma((2, 16)),
            dma((3,)),
            dma((3,)),
            dma,
            dma,
            dma,
            dma,
            dma,
            dma,
            dma,
            dma,
            dma((2, 4)),
            dma((2, 8)),
        ],
        compiler_params=pltpu.CompilerParams(
            collective_id=0, has_side_effects=True, vmem_limit_bytes=48 * 1024 * 1024
        ),
    )(
        *(
            pltpu.with_memory_space_constraint(operand, pltpu.HBM)
            for operand in (
                steps_t,
                noise_gen[0],
                noise_add[0],
                gen_in,
                gen_out.T,
                real_in,
                table(real_qkv),
                real_proj[0],
                real_head.T,
                fake_in,
                table(fake_qkv),
                fake_proj[0],
                fake_head.T,
            )
        )
    )
    dmd, grad_in, grad_out = pl.pallas_call(
        unpack,
        out_shape=(
            jax.ShapeDtypeStruct((32, 64), F32),
            jax.ShapeDtypeStruct((64, 160), F32),
            jax.ShapeDtypeStruct((64, 160), F32),
        ),
        in_specs=[vmem],
        out_specs=(vmem, vmem, vmem),
    )(pltpu.with_memory_space_constraint(packed, pltpu.VMEM))
    return dmd[None], grad_in, grad_out.T


def solution(mesh):
    return jax.shard_map(
        body,
        mesh=mesh,
        in_specs=(
            P("mp", "seq", None),
            P("mp", "seq", None),
            P(),
            P(),
            P(),
            P(),
            P("mp", None, "seq", None),
            P("seq", None, "mp"),
            P(),
            P(),
            P("mp", None, "seq", None),
            P("seq", None, "mp"),
            P(),
        ),
        out_specs=(P("mp", "seq", None), P(None, "seq"), P("seq", None)),
        check_vma=False,
    )
```

```python
import functools
import math

import jax
import jax.numpy as jnp
from jax import lax
from jax.experimental import pallas as pl
from jax.experimental.pallas import tpu as pltpu
from jax.sharding import PartitionSpec as P

MESH = pl.DeviceIdType.MESH
F32 = jnp.float32
BF16 = jnp.bfloat16
NN = (((1,), (0,)), ((), ()))
NT = (((1,), (1,)), ((), ()))
HIGH = lax.Precision.HIGHEST
SCORE_SCALE = math.log2(math.e) / math.sqrt(128.0)
LOSS_SCALE = 1.0 / math.sqrt(8192.0)


def mm(a, b, dims=NN, precision=None):
    return lax.dot_general(a, b, dims, precision=precision, preferred_element_type=F32)


def lanes(shape):
    return lax.broadcasted_iota(jnp.int32, shape, len(shape) - 1)


def roll(value, shift):
    return pltpu.roll(value, shift, 1)


def fold(square):
    return jnp.concatenate([square[0:32], square[32:64]], axis=1)


def kernel(
    steps,
    noise_gen,
    noise_add,
    gen_in,
    gen_out,
    real_in,
    real_qkv,
    real_proj,
    real_head,
    fake_in,
    fake_qkv,
    fake_proj,
    fake_head,
    fin,
    steps_s,
    ngen_v,
    nadd_v,
    gin_v,
    gout_v,
    emb_v,
    head_v,
    qkv_v,
    proj_v,
    embs_v,
    heads_v,
    job_send,
    job_recv,
    ac,
    msg,
    msg_r,
    tok,
    noi,
    keys,
    vals_t,
    scores,
    hid,
    dsil,
    vel,
    vel_r,
    sca,
    gpart,
    grecv,
    load_sem,
    job_ssem,
    job_rsem,
    z_ssem,
    z_rsem,
    ac_ssem,
    ac_rsem,
    core_ssem,
    core_rsem,
    tokz_ssem,
    tokz_rsem,
    tok_ssem,
    tok_rsem,
    noi_ssem,
    noi_rsem,
    sca_ssem,
    sca_rsem,
    g_ssem,
    g_rsem,
):
    mp = lax.axis_index("mp")
    seq = lax.axis_index("seq")
    core = mp & 1
    zlo = mp >> 1
    x = seq >> 3
    zhi = (seq >> 2) & 1
    y = seq & 3
    me_p = x * 4 + y

    def dev(x_, y_, zhi_, zlo_, core_):
        return (zlo_ * 2 + core_, x_ * 8 + zhi_ * 4 + y_)

    def gray(v):
        return v ^ (v >> 1)

    def plane_dev(k):
        near = 15 - k
        return dev((x + gray(near >> 2)) & 3, (y + gray(near & 3)) & 3, zhi, zlo, core)

    partner = dev(x, y, zhi, zlo, 1 - core)
    across = dev(x, y, 1 - zhi, zlo, core)

    def rc(src, dst, ssem, rsem, device):
        return pltpu.make_async_remote_copy(
            src_ref=src, dst_ref=dst, send_sem=ssem, recv_sem=rsem, device_id=device, device_id_type=MESH
        )

    def to_plane(src, dst, ssem, rsem):
        def send(k, carry):
            rc(src, dst, ssem, rsem, plane_dev(k)).start()
            return carry

        lax.fori_loop(0, 15, send, 0, unroll=True)

    def got(ref, rsem):
        rc(ref, ref, rsem, rsem, partner).wait_recv()

    def sent(ref, ssem):
        rc(ref, ref, ssem, ssem, partner).wait_send()

    row = pl.ds(pl.multiple_of(mp * 640, 128), 640)
    loads = [
        pltpu.make_async_copy(real_in.at[:, row], embs_v.at[0], load_sem.at[0]),
        pltpu.make_async_copy(real_qkv, qkv_v.at[0], load_sem.at[1]),
        pltpu.make_async_copy(real_head.at[:, row], heads_v.at[0], load_sem.at[2]),
        pltpu.make_async_copy(real_proj, proj_v.at[0], load_sem.at[3]),
        pltpu.make_async_copy(fake_in.at[:, row], embs_v.at[1], load_sem.at[4]),
        pltpu.make_async_copy(fake_qkv, qkv_v.at[1], load_sem.at[5]),
        pltpu.make_async_copy(fake_head.at[:, row], heads_v.at[1], load_sem.at[6]),
        pltpu.make_async_copy(fake_proj, proj_v.at[1], load_sem.at[7]),
        pltpu.make_async_copy(gen_in, gin_v, load_sem.at[8]),
        pltpu.make_async_copy(gen_out, gout_v, load_sem.at[9]),
        pltpu.make_async_copy(noise_gen, ngen_v, load_sem.at[12]),
        pltpu.make_async_copy(noise_add, nadd_v, load_sem.at[13]),
        pltpu.make_async_copy(steps, steps_s, load_sem.at[14]),
    ]
    for load in loads:
        load.start()

    @pl.when(core == 0)
    def _():
        pltpu.make_async_copy(real_in, emb_v, load_sem.at[10]).start()
        pltpu.make_async_copy(real_head, head_v, load_sem.at[11]).start()

    @pl.when(core == 1)
    def _():
        pltpu.make_async_copy(fake_in, emb_v, load_sem.at[10]).start()
        pltpu.make_async_copy(fake_head, head_v, load_sem.at[11]).start()

    barrier = pltpu.get_barrier_semaphore()

    def greet(device):
        pl.semaphore_signal(barrier, inc=1, device_id=device, device_id_type=MESH)

    def greet_plane(k, carry):
        greet(plane_dev(k))
        return carry

    def greet_mp(k, carry):
        greet(((mp + k) & 7, seq))
        return carry

    def greet_across(k, carry):
        greet(dev(x, y, 1 - zhi, k, core))
        return carry

    lax.fori_loop(0, 4, greet_across, 0, unroll=True)
    lax.fori_loop(0, 15, greet_plane, 0, unroll=True)
    lax.fori_loop(1, 8, greet_mp, 0, unroll=True)

    for m in range(2):
        for k in range(4):
            loads[4 * m + k].wait()
        for c in range(3):
            job_send[2 * m + c // 2, :, (c % 2) * 128 : (c % 2) * 128 + 128] = mm(embs_v[m], qkv_v[m, c]).astype(BF16)
        job_send[2 * m + 1, :, 128:256] = mm(heads_v[m], proj_v[m], NT).astype(BF16)

    for k in range(8, 13):
        loads[k].wait()
    level = steps_s[zlo].astype(F32) / 1000.0
    own_noise = ngen_v[...]
    clean = own_noise.astype(F32)
    for c in range(5):
        cols = slice(c * 1024, c * 1024 + 1024)
        u = mm(own_noise, gin_v[:, cols])
        hidden = (u * jax.nn.sigmoid(u)).astype(BF16)
        clean = clean + mm(hidden, gout_v[:, cols], NT)
    noised = (1.0 - level) * clean + level * nadd_v[...].astype(F32)
    msg[...] = jnp.concatenate([noised, own_noise.astype(F32)], axis=1).astype(BF16)

    scores[...] = jnp.zeros((2, 2048, 512), F32)
    pl.semaphore_wait(barrier, 26)

    for m in range(2):
        for t in range(2):

            @pl.when(jnp.logical_not((zlo == 1 + t) & (core == m)))
            def _(m=m, t=t):
                rc(
                    job_send.at[2 * m + t],
                    job_recv.at[mp],
                    job_ssem.at[2 * m + t],
                    job_rsem.at[mp],
                    dev(x, y, zhi, 1 + t, m),
                ).start()

    rc(msg, msg_r, core_ssem.at[0], core_rsem.at[0], partner).start()
    got(msg_r, core_rsem.at[0])
    left = lanes((32, 128)) < 64
    mine = msg[...].astype(F32)
    other = msg_r[...].astype(F32)
    half0 = jnp.where(core == 0, mine, other)
    half1 = jnp.where(core == 0, other, mine)
    own_tok = jnp.where(left, half0, roll(half1, 64))
    tok[zhi, me_p] = own_tok.astype(BF16)
    noi[me_p] = jnp.where(left, roll(half0, 64), half1).astype(BF16)
    own_ref = tok.at[zhi, me_p]
    rc(own_ref, own_ref, tokz_ssem, tokz_rsem, across).start()
    to_plane(own_ref, own_ref, tok_ssem, tok_rsem)
    xtok = jnp.concatenate([own_tok[:, 0:64], own_tok[:, 64:128]], axis=0)
    xcol = xtok.T.astype(BF16)
    xzero = jnp.zeros((64, 64), BF16)
    xpair = jnp.concatenate(
        [jnp.concatenate([xcol, xzero], axis=1), jnp.concatenate([xzero, xcol], axis=1)], axis=0
    )
    noi_ref = noi.at[me_p]
    to_plane(noi_ref, noi_ref, noi_ssem, noi_rsem)

    pltpu.make_async_copy(real_in, emb_v, load_sem.at[10]).wait()
    pltpu.make_async_copy(real_head, head_v, load_sem.at[11]).wait()
    direct = mm(emb_v[...], head_v[...], NT)
    vel[...] = mm(xtok, direct, precision=HIGH)

    t_here = zlo - 1
    slot_here = zhi * 2 + t_here

    @pl.when((zlo == 1) | (zlo == 2))
    def _():
        total = job_send[core * 2 + t_here].astype(F32)
        for src in range(8):

            @pl.when(src != mp)
            def _(src=src):
                got(job_recv.at[src], job_rsem.at[src])

            @pl.when(src == mp)
            def _(src=src):
                job_recv[src] = jnp.zeros((64, 256), BF16)

            total = total + job_recv[src].astype(F32)
        scale = jnp.where(t_here == 0, SCORE_SCALE, 1.0).astype(F32)
        square = mm(total[:, 128:256], total[:, 0:128], NT, HIGH) * scale
        ac[me_p, slot_here] = fold(square).astype(BF16)
        piece = ac.at[me_p, slot_here]

        def spread(k, carry):
            z = (zhi * 4 + zlo + k) & 7
            rc(piece, piece, z_ssem, z_rsem.at[slot_here], dev(x, y, z >> 2, z & 3, core)).start()
            return carry

        lax.fori_loop(1, 8, spread, 0, unroll=True)

    far_ref = tok.at[1 - zhi, me_p]
    got(far_ref, tokz_rsem)
    to_plane(far_ref, far_ref, tok_ssem, tok_rsem)

    upper = zlo // 2
    for order in range(4):
        group = zhi if order < 2 else 1 - zhi
        t = upper if order in (0, 3) else 1 - upper
        slot = group * 2 + t
        piece = ac.at[me_p, slot]

        @pl.when(jnp.logical_not((group == zhi) & (zlo == 1 + t)))
        def _(piece=piece, slot=slot):
            got(piece, z_rsem.at[slot])

        to_plane(piece, piece, ac_ssem, ac_rsem.at[group, me_p])

    got(tok.at[0:2, 0:15], tok_rsem)
    for g in range(2):
        block = tok[g].reshape(512, 128).astype(F32)
        flipped = block.T.astype(BF16)
        rows0 = slice(g * 512, g * 512 + 512)
        rows1 = slice(1024 + g * 512, 1024 + g * 512 + 512)
        vals_t[0:64, rows0] = flipped[0:64]
        vals_t[0:64, rows1] = flipped[64:128]
        keys[rows0, :] = block[:, 0:64].astype(BF16)
        keys[rows1, :] = roll(block, 64)[:, 0:64].astype(BF16)
    vals_t[64:80, :] = jnp.ones((16, 2048), BF16)

    near = ((0, 0), (0, 1), (0, 3), (1, 0), (3, 0), (0, 2), (1, 1), (3, 3))
    far = ((1, 3), (3, 1), (2, 0), (1, 2), (3, 2), (2, 1), (2, 3), (2, 2))

    def spots(b):
        return [((x + kx) & 3) * 4 + ((y + ky) & 3) for kx, ky in (near if b % 2 == 0 else far)]

    def group_of(b):
        return zhi if b < 2 else 1 - zhi

    def pairs(b, t):
        slot = 2 * group_of(b) + t
        here = spots(b)
        return [(ac[here[i], slot].astype(F32), ac[here[i + 1], slot].astype(F32)) for i in (0, 2, 4, 6)]

    def queries(b):
        for spot in spots(b)[1 if b % 2 == 0 else 0 :]:
            got(ac.at[spot, pl.ds(2 * group_of(b), 2)], ac_rsem.at[group_of(b), spot])
        out = []
        for f0, f1 in pairs(b, 0):
            upper_rows = jnp.where(left, f0, roll(f1, 64))
            lower_rows = jnp.where(left, roll(f0, 64), f1)
            mats = jnp.concatenate([upper_rows, lower_rows], axis=0).astype(BF16)
            out.append(mm(mats, xpair).astype(BF16))
        return jnp.concatenate(out, axis=1)

    def score_chunk(b, q, j, top):
        rows = slice(j * 256, j * 256 + 256)
        s = mm(keys[rows, :], q)
        scores[b % 2, rows, :] = s
        here = jnp.max(s.reshape(32, 8, 512), axis=0)
        return here if top is None else jnp.maximum(top, here)

    def value_chunk(b, top, j, total):
        rows = slice(j * 256, j * 256 + 256)
        weights = jnp.exp2(scores[b % 2, rows, :] - top).astype(BF16)
        part = mm(vals_t[:, rows], weights)
        return part if total is None else total + part

    def finish(b, total, acc):
        mixed = (total[0:64] / total[64:65]).astype(BF16)
        for i, (f0, f1) in enumerate(pairs(b, 1)):
            mats = jnp.concatenate([f0, roll(f0, 64), f1, roll(f1, 64)], axis=0)[:, 0:64].astype(BF16)
            acc = acc + mm(mats, mixed[:, i * 128 : i * 128 + 128])
        return acc

    acc = jnp.zeros((128, 128), F32)
    for b in range(4):
        if b in (0,):
            q = queries(b)
            top = None
            for j in range(8):
                top = score_chunk(b, q, j, top)
        peak = jnp.max(top, axis=0, keepdims=True)
        if b in (0, 1, 2):
            q = queries(b + 1)
        top = None
        total = None
        for j in range(8):
            if b in (0, 1, 2):
                top = score_chunk(b + 1, q, j, top)
            total = value_chunk(b, peak, j, total)
        acc = finish(b, total, acc)
    total_vel = vel[...] + (acc[0:64, 0:64] + acc[64:128, 64:128]).T
    vel_fold = jnp.concatenate([total_vel[0:32], total_vel[32:64]], axis=1)
    sca_f = vel_fold
    fin[0:32, :] = sca_f
    rc(fin.at[0:32], vel_r, core_ssem.at[1], core_rsem.at[1], partner).start()

    got(noi.at[0:15], noi_rsem)
    col0 = 160 * (x * 8 + core * 4 + y)
    base = pl.ds(pl.multiple_of((col0 // 128) * 128, 128), 256)
    shift = 256 - 32 * y
    gin_s = pltpu.roll(gin_v[:, base].astype(F32), shift, 1).astype(BF16)
    gout_s = pltpu.roll(gout_v[:, base].astype(F32), shift, 1).astype(BF16)
    zeros = jnp.zeros((64, 256), BF16)
    noise_rows = noi[...].reshape(512, 128)
    for h in range(2):
        weight = jnp.concatenate([gin_s, zeros] if h == 0 else [zeros, gin_s], axis=0)
        u = mm(noise_rows, weight)
        sig = jax.nn.sigmoid(u)
        hid[h] = (u * sig).astype(BF16)
        dsil[h] = sig * (1.0 + u * (1.0 - sig))
    noise_t = noise_rows.astype(F32).T.astype(BF16)

    got(vel_r, core_rsem.at[1])
    sign = jnp.where(core == 0, 1.0, -1.0).astype(F32)
    dmd = level * (sign * (vel_fold - vel_r[...]))
    dmd_full = jnp.where(core == 0, dmd, roll(dmd, 64))
    sca[me_p] = (dmd * LOSS_SCALE).astype(BF16)
    sca_ref = sca.at[me_p]
    to_plane(sca_ref, sca_ref, sca_ssem, sca_rsem)
    got(sca.at[0:15], sca_rsem)

    scaled_rows = sca[...].reshape(512, 128)
    scaled_t = scaled_rows.astype(F32).T.astype(BF16)
    grad_in = jnp.zeros((64, 256), F32)
    grad_out = jnp.zeros((64, 256), F32)
    for h in range(2):
        grad_out = grad_out + mm(scaled_t[h * 64 : h * 64 + 64], hid[h])
        weight = jnp.concatenate([gout_s, zeros] if h == 0 else [zeros, gout_s], axis=0)
        pre = (mm(scaled_rows, weight) * dsil[h]).astype(BF16)
        grad_in = grad_in + mm(noise_t[h * 64 : h * 64 + 64], pre)
    grads = jnp.concatenate([grad_in, grad_out], axis=0)
    lane32 = lanes((32, 128))
    rest = grads[0:32, 128:256]
    for i in range(1, 4):
        rest = jnp.where(lane32 < 32 * i, rest, roll(grads[32 * i : 32 * i + 32, 128:256], 32 * i))
    gpart[0:128, :] = grads[:, 0:128].astype(BF16)
    gpart[128:160, :] = rest.astype(BF16)

    sent(fin.at[0:32], core_ssem.at[1])
    fin[0:32, :] = dmd_full

    zme = zhi * 4 + zlo
    for k in range(4):

        @pl.when(jnp.logical_not((zhi == core) & (zlo == k)))
        def _(k=k):
            rc(gpart, grecv.at[zme], g_ssem.at[k], g_rsem.at[zme], dev(x, y, core, k, core)).start()

    @pl.when(zhi == core)
    def _():
        total = gpart[...].astype(F32)
        for src in range(8):

            @pl.when(src != zme)
            def _(src=src):
                got(grecv.at[src], g_rsem.at[src])

            @pl.when(src == zme)
            def _(src=src):
                grecv[src] = jnp.zeros((160, 128), BF16)

            total = total + grecv[src].astype(F32)
        fin[32:192, :] = total
        rc(fin.at[32:192], fin.at[32:192], core_ssem.at[2], core_rsem.at[2], partner).start()

    @pl.when(zhi != core)
    def _():
        got(fin.at[32:192], core_rsem.at[2])

    for m in range(2):
        for t in range(2):

            @pl.when(jnp.logical_not((zlo == 1 + t) & (core == m)))
            def _(m=m, t=t):
                sent(job_send.at[2 * m + t], job_ssem.at[2 * m + t])

    @pl.when((zlo == 1) | (zlo == 2))
    def _():
        sent(noi.at[0:7], z_ssem)

    for k in range(4):

        @pl.when(jnp.logical_not((zhi == core) & (zlo == k)))
        def _(k=k):
            sent(gpart, g_ssem.at[k])

    @pl.when(zhi == core)
    def _():
        sent(fin.at[32:192], core_ssem.at[2])

    sent(msg, core_ssem.at[0])
    sent(own_ref, tokz_ssem)
    sent(tok.at[0:2, 0:15], tok_ssem)
    sent(ac.at[0:15], ac_ssem)
    sent(noi.at[0:15], noi_ssem)
    sent(sca.at[0:15], sca_ssem)


def unpack(packed, dmd_out, gin_out, gout_out):
    dmd_out[...] = packed[0:32, 0:64]
    gin_out[:, 0:128] = packed[32:96, :]
    gout_out[:, 0:128] = packed[96:160, :]
    tail = packed[160:192, :]
    for i in range(4):
        ref = gin_out if i < 2 else gout_out
        piece = tail if i == 0 else roll(tail, 128 - 32 * i)
        ref[(i % 2) * 32 : (i % 2) * 32 + 32, 128:160] = piece[:, 0:32]


def body(
    noise_gen,
    noise_add,
    steps_t,
    gen_in,
    gen_out,
    real_in,
    real_qkv,
    real_proj,
    real_head,
    fake_in,
    fake_qkv,
    fake_proj,
    fake_head,
):
    def table(qkv):
        return qkv.transpose(1, 2, 0, 3).reshape(3, 640, 128)

    vmem = pl.BlockSpec(memory_space=pltpu.VMEM)
    hbm = pl.BlockSpec(memory_space=pltpu.HBM)
    dma = pltpu.SemaphoreType.DMA
    packed = pl.pallas_call(
        kernel,
        out_shape=jax.ShapeDtypeStruct((192, 128), F32),
        in_specs=[hbm] * 13,
        out_specs=vmem,
        scratch_shapes=[
            pltpu.SMEM((4,), jnp.int32),
            pltpu.VMEM((32, 64), BF16),
            pltpu.VMEM((32, 64), BF16),
            pltpu.VMEM((64, 5120), BF16),
            pltpu.VMEM((64, 5120), BF16),
            pltpu.VMEM((64, 5120), BF16),
            pltpu.VMEM((64, 5120), BF16),
            pltpu.VMEM((2, 3, 640, 128), BF16),
            pltpu.VMEM((2, 128, 640), BF16),
            pltpu.VMEM((2, 64, 640), BF16),
            pltpu.VMEM((2, 64, 640), BF16),
            pltpu.VMEM((4, 64, 256), BF16),
            pltpu.VMEM((8, 64, 256), BF16),
            pltpu.VMEM((16, 4, 32, 128), BF16),
            pltpu.VMEM((32, 128), BF16),
            pltpu.VMEM((32, 128), BF16),
            pltpu.VMEM((2, 16, 32, 128), BF16),
            pltpu.VMEM((16, 32, 128), BF16),
            pltpu.VMEM((2048, 64), BF16),
            pltpu.VMEM((80, 2048), BF16),
            pltpu.VMEM((2, 2048, 512), F32),
            pltpu.VMEM((2, 512, 256), BF16),
            pltpu.VMEM((2, 512, 256), F32),
            pltpu.VMEM((64, 64), F32),
            pltpu.VMEM((32, 128), F32),
            pltpu.VMEM((16, 32, 128), BF16),
            pltpu.VMEM((160, 128), BF16),
            pltpu.VMEM((8, 160, 128), BF16),
            dma((15,)),
            dma((4,)),
            dma((8,)),
            dma,
            dma((4,)),
            dma,
            dma((2, 16)),
            dma((3,)),
            dma((3,)),
            dma,
            dma,
            dma,
            dma,
            dma,
            dma,
            dma,
            dma,
            dma((4,)),
            dma((8,)),
        ],
        compiler_params=pltpu.CompilerParams(
            collective_id=0, has_side_effects=True, vmem_limit_bytes=48 * 1024 * 1024
        ),
    )(
        *(
            pltpu.with_memory_space_constraint(operand, pltpu.HBM)
            for operand in (
                steps_t,
                noise_gen[0],
                noise_add[0],
                gen_in,
                gen_out.T,
                real_in,
                table(real_qkv),
                real_proj[0],
                real_head.T,
                fake_in,
                table(fake_qkv),
                fake_proj[0],
                fake_head.T,
            )
        )
    )
    dmd, grad_in, grad_out = pl.pallas_call(
        unpack,
        out_shape=(
            jax.ShapeDtypeStruct((32, 64), F32),
            jax.ShapeDtypeStruct((64, 160), F32),
            jax.ShapeDtypeStruct((64, 160), F32),
        ),
        in_specs=[vmem],
        out_specs=(vmem, vmem, vmem),
    )(pltpu.with_memory_space_constraint(packed, pltpu.VMEM))
    return dmd[None], grad_in, grad_out.T


def solution(mesh):
    return jax.shard_map(
        body,
        mesh=mesh,
        in_specs=(
            P("mp", "seq", None),
            P("mp", "seq", None),
            P(),
            P(),
            P(),
            P(),
            P("mp", None, "seq", None),
            P("seq", None, "mp"),
            P(),
            P(),
            P("mp", None, "seq", None),
            P("seq", None, "mp"),
            P(),
        ),
        out_specs=(P("mp", "seq", None), P(None, "seq"), P("seq", None)),
        check_vma=False,
    )
```
